512 devices in a mesh: wide: 64 (over z_hi, y, core), narrow: 8 (over x, z_lo).
Axes of the slice: x: 4, y: 8, z: 8 (z_hi: 4, z_lo: 2; z = z_hi * 2 + z_lo), core: 2. Of those that a mesh axis runs over, the one named last changes fastest.
Arguments:
- teacher_in: bfloat16 [512, 6144], P('wide', 'narrow')
- teacher_gain: bfloat16 [6144], P('narrow'), may hold values from 0.5 to 1.5
- mlp_in: bfloat16 [6144, 24576], P('narrow', 'wide'), may hold values from -0.078125 to 0.078125
- mlp_out: bfloat16 [24576, 6144], P('wide', 'narrow'), may hold values from -0.0390625 to 0.0390625
- projector: bfloat16 [6144, 1024], P('narrow', 'wide'), may hold values from -0.078125 to 0.078125
- student_in: bfloat16 [256, 256, 1024], P('wide')
- sample_pos: int32 [256, 2], P('wide'), may hold values from 0 to 255, as said below
- w_qkv: bfloat16 [3, 1024, 1024], P(None, None, 'narrow')
- w_attn_out: bfloat16 [1024, 1024], P('narrow'), may hold values from -0.1875 to 0.1875
Outputs:
- grad_qkv: float32 [3, 1024, 1024], P(None, 'wide', 'narrow')
- grad_attn_out: float32 [1024, 1024], P('narrow', 'wide')
- grad_projector: float32 [6144, 1024], P('narrow', 'wide')
The draws below stay inside these ranges and needn't reach their ends.
Inputs may be any that keep to these rules, and one draw needn't show every extreme that they name: `sample_pos`: position j of an image lies in [j * 128, (j + 1) * 128).
All inputs are finite; a program needn't handle non-finite values.
Results may differ from the reference program's by a relative error of at most 0.012.
Values may be sent and summed in bfloat16 or wider, within the bound.
No kernel may reach another device: no remote copies, remote signals or barrier semaphores. Data moves between devices by JAX's collectives and lax.ppermute only.
A program may use at most 64 MiB of HBM per device.

```python
import math
import jax
import jax.numpy as jnp
from jax import lax

D_T = 6144
FF_T = 24576
D_S = 1024
HEADS_S = 16
HEAD_DIM = 64
PATCHES = 256
SEL = 2
IMG_DEV = 4
IMAGES = 256
TSEL = 512


def draw_teacher_in(key, part):
    key = jax.random.fold_in(key, 11)
    first, second, third = jax.random.split(key, 3)
    columns = jnp.arange(D_T, dtype=jnp.float32) / max(D_T - 1, 1)
    trend = jnp.exp(math.log(3.0) * (columns - 0.5))[None, :]
    base = jax.random.normal(first, (TSEL, D_T), jnp.float32)
    row_scale = jnp.exp(jax.random.uniform(second, (TSEL, 1), jnp.float32, math.log(0.3), math.log(3.0)))
    column_scale = jnp.exp(jax.random.uniform(third, (1, D_T), jnp.float32, math.log(0.3), math.log(3.0))) * trend
    return (base * row_scale * column_scale).astype(jnp.bfloat16)


def draw_student_in(key, part):
    key = jax.random.fold_in(key, 12)
    first, second = jax.random.split(key, 2)
    row_scale = jnp.exp(jax.random.uniform(second, (IMAGES, PATCHES, 1), jnp.float32, math.log(0.5), math.log(2.0)))
    base = jax.random.normal(first, (IMAGES, PATCHES, D_S), jnp.float32)
    return (base * row_scale).astype(jnp.bfloat16)


def draw_w_qkv(key, part):
    key = jax.random.fold_in(key, 13)
    first = jax.random.fold_in(key, 0)
    return (jax.random.normal(first, (3, D_S, D_S), jnp.float32) / math.sqrt(D_S)).astype(jnp.bfloat16)


def draw_sample_pos(key, part):
    key = jax.random.fold_in(key, 14)
    first, second, third = jax.random.split(key, 3)
    stride = PATCHES // SEL
    offset = jax.random.randint(first, (IMAGES, SEL), 0, stride, dtype=jnp.int32)
    low_image = jax.random.randint(second, (), 0, IMAGES, dtype=jnp.int32)
    high_image = jax.random.randint(third, (), 0, IMAGES, dtype=jnp.int32)
    offset = offset.at[low_image, 0].set(0)
    offset = offset.at[high_image, SEL - 1].set(stride - 1)
    return (jnp.arange(SEL, dtype=jnp.int32)[None, :] * stride + offset).astype(jnp.int32)


def steps_of(own_key, shape, cuts, least, high):
    loudness = 1.0
    for dim, parts in cuts:
        draws = jax.random.uniform(jax.random.fold_in(jax.random.fold_in(own_key, 6), dim), (parts,), jnp.float32, least / len(cuts), high / len(cuts))
        loudness = loudness * jnp.repeat(jnp.exp(draws), shape[dim] // parts).reshape((-1,) + (1,) * (len(shape) - 1 - dim))
    return loudness


def scatter_about(rng, extent, width, most, pieces=(), held_as=jnp.bfloat16):
    factor_of = steps_of(rng, extent, pieces, -0.22, 0.18) if pieces else 1.0
    result = jax.random.normal(rng, extent, jnp.float32) * width * factor_of
    return jnp.minimum(jnp.maximum(result, -most), most).astype(held_as)


def setup_inputs(seed: int = 0) -> dict:
    seeds = jax.random.split(jax.random.key(seed), 10)
    teacher_in = draw_teacher_in(jax.random.fold_in(seeds[9], 71), 0)
    teacher_gain = jnp.clip(1.0 + 0.1 * jax.random.normal(seeds[1], (D_T,), jnp.float32), 0.5, 1.5).astype(jnp.bfloat16)
    mlp_in = scatter_about(seeds[2], (D_T, FF_T), D_T ** -0.5, 0.078125, ((0, 8), (1, 64)))
    mlp_out = scatter_about(seeds[3], (FF_T, D_T), FF_T ** -0.5, 0.0390625, ((0, 64), (1, 8)))
    projector = scatter_about(seeds[4], (D_T, D_S), D_T ** -0.5, 0.078125, ((0, 8), (1, 64)))
    student_in = draw_student_in(jax.random.fold_in(seeds[9], 71), 0)
    sample_pos = draw_sample_pos(jax.random.fold_in(seeds[9], 71), 0)
    w_qkv = draw_w_qkv(jax.random.fold_in(seeds[9], 71), 0)
    w_attn_out = scatter_about(seeds[8], (D_S, D_S), D_S ** -0.5, 0.1875, ((0, 8),))
    return dict(teacher_in=teacher_in, teacher_gain=teacher_gain, mlp_in=mlp_in, mlp_out=mlp_out, projector=projector, student_in=student_in, sample_pos=sample_pos, w_qkv=w_qkv, w_attn_out=w_attn_out)


def reference(teacher_in, teacher_gain, mlp_in, mlp_out, projector, student_in, sample_pos, w_qkv, w_attn_out):
    f32 = jnp.float32
    bf16 = jnp.bfloat16
    wide_in = teacher_in.astype(f32)
    center = lax.optimization_barrier(jnp.mean(wide_in, axis=-1, keepdims=True))
    spread = lax.optimization_barrier(jnp.mean(wide_in * wide_in, axis=-1, keepdims=True)) - center * center
    normed = ((wide_in - center) * lax.rsqrt(spread + 1e-06) * teacher_gain.astype(f32)).astype(bf16)
    pre = jnp.dot(normed, mlp_in, preferred_element_type=f32)
    hidden = jax.nn.gelu(pre, approximate=False).astype(bf16)
    teacher_out = (wide_in + jnp.dot(hidden, mlp_out, preferred_element_type=f32)).astype(bf16)
    target = jnp.dot(teacher_out, projector, preferred_element_type=f32)
    source = student_in.astype(f32)
    center_s = lax.optimization_barrier(jnp.mean(source, axis=-1, keepdims=True))
    spread_s = lax.optimization_barrier(jnp.mean(source * source, axis=-1, keepdims=True)) - center_s * center_s
    student_norm = ((source - center_s) * lax.rsqrt(spread_s + 1e-06)).astype(bf16)
    flat_norm = student_norm.reshape(IMAGES * PATCHES, D_S)
    keys = jnp.dot(flat_norm, w_qkv[1], preferred_element_type=f32).astype(bf16).reshape(IMAGES, PATCHES, HEADS_S, HEAD_DIM)
    values = jnp.dot(flat_norm, w_qkv[2], preferred_element_type=f32).astype(bf16).reshape(IMAGES, PATCHES, HEADS_S, HEAD_DIM)
    index = sample_pos.astype(jnp.int32)[:, :, None]
    picked_norm = jnp.take_along_axis(student_norm, index, axis=1).reshape(TSEL, D_S)
    picked_in = jnp.take_along_axis(student_in, index, axis=1).reshape(TSEL, D_S).astype(f32)
    queries = jnp.dot(picked_norm, w_qkv[0], preferred_element_type=f32).astype(bf16).reshape(IMAGES, SEL, HEADS_S, HEAD_DIM)
    scale = HEAD_DIM ** (-0.5)
    scores = jnp.einsum('ishd,iphd->ihsp', queries.astype(f32), keys.astype(f32)) * scale
    probs = jax.nn.softmax(scores, axis=-1)
    probs_low = probs.astype(bf16)
    context = jnp.einsum('ihsp,iphd->ishd', probs_low.astype(f32), values.astype(f32)).astype(bf16).reshape(TSEL, D_S)
    student_out = picked_in + jnp.dot(context, w_attn_out, preferred_element_type=f32)
    delta = ((student_out - target) / (SEL * IMG_DEV)).astype(bf16)
    grad_projector = -jnp.dot(teacher_out.T, delta, preferred_element_type=f32)
    grad_attn_out = jnp.dot(context.T, delta, preferred_element_type=f32)
    d_context = jnp.dot(delta, w_attn_out.T, preferred_element_type=f32).astype(bf16).reshape(IMAGES, SEL, HEADS_S, HEAD_DIM)
    d_probs = jnp.einsum('ishd,iphd->ihsp', d_context.astype(f32), values.astype(f32))
    d_scores = (probs * (d_probs - lax.optimization_barrier(jnp.sum(probs * d_probs, axis=-1, keepdims=True))) * scale).astype(bf16)
    d_query = jnp.einsum('ihsp,iphd->ishd', d_scores.astype(f32), keys.astype(f32)).astype(bf16).reshape(TSEL, D_S)
    d_key = jnp.einsum('ihsp,ishd->iphd', d_scores.astype(f32), queries.astype(f32)).astype(bf16).reshape(IMAGES * PATCHES, D_S)
    d_value = jnp.einsum('ihsp,ishd->iphd', probs_low.astype(f32), d_context.astype(f32)).astype(bf16).reshape(IMAGES * PATCHES, D_S)
    grad_query = jnp.dot(picked_norm.T, d_query, preferred_element_type=f32)
    grad_key = jnp.dot(flat_norm.T, d_key, preferred_element_type=f32)
    grad_value = jnp.dot(flat_norm.T, d_value, preferred_element_type=f32)
    return (jnp.stack([grad_query, grad_key, grad_value]), grad_attn_out, grad_projector)
```

```python
import jax
import jax.numpy as jnp
from jax import lax
from jax.sharding import PartitionSpec as P

HEAD_DIM = 64
LANES = 128
EPSILON = 1e-06
Z_PARTS = 4
CORES = 2

f32 = jnp.float32
bf16 = jnp.bfloat16


def product(left, right, dims=((1,), (0,))):
    return lax.dot_general(left, right, (dims, ((), ())), preferred_element_type=f32)


def wide_groups(z_parts, y_parts, cores):
    def place(z, y, c):
        return (z * y_parts + y) * cores + c

    zs, ys, cs = range(z_parts), range(y_parts), range(cores)
    along_z = [[place(z, y, c) for z in zs] for y in ys for c in cs]
    along_y = [[place(z, y, c) for y in ys] for z in zs for c in cs]
    along_c = [[place(z, y, c) for c in cs] for z in zs for y in ys]
    return along_z, along_y, along_c


def exchange(block, axis, groups=None):
    return lax.all_to_all(block, axis, 0, 0, axis_index_groups=groups)


def spread(block, axis, count, groups=None):
    return exchange(jnp.broadcast_to(block[None], (count,) + block.shape), axis, groups)


def make_local(wide, narrow, z_parts, cores):
    y_parts = wide // (z_parts * cores)
    along_z, along_y, along_c = wide_groups(z_parts, y_parts, cores)

    def gather_rows(block):
        for groups in (along_z, along_y, along_c):
            block = lax.all_gather(block, "wide", axis_index_groups=groups, tiled=True)
        return block

    def spread_rows(block):
        width = block.shape[1]
        for groups in (along_z, along_y, along_c):
            block = spread(block, "wide", len(groups[0]), groups).reshape(-1, width)
        return block

    def sum_to_owners(partial):
        width = partial.shape[1]
        for groups, kind in ((along_c, bf16), (along_y, bf16), (along_z, f32)):
            count = len(groups[0])
            block = partial.astype(kind).reshape(count, -1, width)
            partial = jnp.sum(exchange(block, "wide", groups).astype(f32), axis=0)
        return partial

    def local(
        teacher_in,
        teacher_gain,
        mlp_in,
        mlp_out,
        projector,
        student_in,
        sample_pos,
        w_qkv,
        w_attn_out,
    ):
        rows, features = teacher_in.shape
        d_t = features * narrow
        images, patches, width = student_in.shape
        select = sample_pos.shape[1]
        local_width = w_qkv.shape[2]
        scale = HEAD_DIM ** (-0.5)
        total_rows = rows * wide

        own = teacher_in.astype(f32)
        sums = jnp.concatenate(
            [
                jnp.sum(own, axis=1, keepdims=True),
                jnp.sum(own * own, axis=1, keepdims=True),
            ],
            axis=1,
        )
        sums = jnp.sum(spread(sums, "narrow", narrow), axis=0)
        center = sums[:, 0:1] / d_t
        variance = sums[:, 1:2] / d_t - center * center
        normed = (
            (own - center) * lax.rsqrt(variance + EPSILON) * teacher_gain.astype(f32)
        ).astype(bf16)
        normed = gather_rows(normed)

        pre = product(normed, mlp_in).astype(bf16)
        pre = exchange(pre.reshape(narrow, total_rows // narrow, -1), "narrow")
        pre = jnp.sum(pre.astype(f32), axis=0)
        hidden = jax.nn.gelu(pre, approximate=False).astype(bf16)
        hidden = spread(hidden, "narrow", narrow).reshape(total_rows, -1)
        branch = sum_to_owners(product(hidden, mlp_out))
        teacher_local = (own + branch).astype(bf16)

        flat_in = student_in.reshape(images * patches, width)
        source = flat_in.astype(f32)
        center_s = jnp.mean(source, axis=-1, keepdims=True)
        spread_s = jnp.mean(source * source, axis=-1, keepdims=True) - center_s * center_s
        flat_norm = ((source - center_s) * lax.rsqrt(spread_s + EPSILON)).astype(bf16)
        keys = product(flat_norm, w_qkv[1]).astype(bf16)
        values = product(flat_norm, w_qkv[2]).astype(bf16)
        picks = images * select
        column = lax.broadcasted_iota(jnp.int32, (picks, images * patches), 1)
        pick_image = lax.broadcasted_iota(jnp.int32, (picks, 1), 0) // select
        wanted = pick_image * patches + sample_pos.reshape(picks, 1)
        chosen = (column == wanted).astype(bf16)
        picked_norm = product(chosen, flat_norm).astype(bf16)
        picked_in = product(chosen, flat_in)
        queries = product(picked_norm, w_qkv[0]).astype(bf16)
        lane_head = lax.broadcasted_iota(jnp.int32, (1, local_width), 1) // HEAD_DIM
        heads_here = local_width // HEAD_DIM

        def by_head(block):
            return jnp.concatenate(
                [jnp.where(lane_head == h, block, 0).astype(bf16) for h in range(heads_here)]
            )

        def merge_heads(block):
            merged = block[:picks]
            for h in range(1, heads_here):
                merged = jnp.where(lane_head == h, block[h * picks : (h + 1) * picks], merged)
            return merged.astype(bf16)

        scores = product(by_head(queries), keys, ((1,), (1,))) * scale
        own_image = jnp.tile(column // patches == pick_image, (heads_here, 1))
        probs = jax.nn.softmax(jnp.where(own_image, scores, -jnp.inf), axis=-1)
        probs_low = probs.astype(bf16)
        context = merge_heads(product(probs_low, values))
        value_side = product(probs_low, flat_norm).astype(bf16)
        mixed = product(context, w_attn_out)

        held = spread_rows(jnp.concatenate([teacher_local, queries, context], axis=1))
        target = product(held[:, :features], projector)
        target = target.reshape(cores, y_parts, z_parts, rows, -1).transpose(2, 1, 0, 3, 4)
        target = exchange(target.reshape(wide, rows, -1), "wide")
        target = target.transpose(1, 0, 2).reshape(rows, -1)
        student_out = picked_in + jnp.sum(spread(mixed - target, "narrow", narrow), axis=0)
        delta = (student_out / (select * images)).astype(bf16)

        d_context = product(delta, w_attn_out, ((1,), (1,))).astype(bf16)
        d_probs = product(by_head(d_context), values, ((1,), (1,)))
        d_scores = (
            probs * (d_probs - jnp.sum(probs * d_probs, axis=-1, keepdims=True)) * scale
        ).astype(bf16)
        d_query = merge_heads(product(d_scores, keys))
        key_side = product(d_scores, flat_norm).astype(bf16)

        factors = jnp.concatenate([delta, picked_norm, key_side, value_side], axis=0)
        kinds = factors.shape[0] // rows
        piece = width // wide
        per_tile = LANES // piece
        tiles = width // LANES
        factors = factors.reshape(kinds, rows, tiles, LANES).transpose(2, 1, 0, 3)
        factors = factors.reshape(tiles * rows, kinds * LANES)
        at_in = lax.broadcasted_iota(jnp.int32, (kinds * LANES, per_tile * LANES), 0)
        at_out = lax.broadcasted_iota(jnp.int32, (kinds * LANES, per_tile * LANES), 1)
        lane_in, kind_in = at_in % LANES, at_in // LANES
        lane_out, tile_out = at_out % LANES, at_out // LANES
        move = (
            (lane_in // piece == tile_out)
            & (lane_out // piece == kind_in)
            & (lane_in % piece == lane_out % piece)
        ).astype(bf16)
        packed = product(factors, move).astype(bf16)
        packed = packed.reshape(tiles, rows, per_tile, LANES).transpose(0, 2, 1, 3)
        packed = packed.reshape(wide, rows, LANES)
        late = jnp.concatenate([d_query, d_context], axis=1)
        late = jnp.broadcast_to(late[None], (wide,) + late.shape)
        got = exchange(jnp.concatenate([packed, late], axis=2), "wide")
        got = got.reshape(z_parts, y_parts, cores, rows, -1).transpose(2, 1, 0, 3, 4)
        got = got.reshape(total_rows, -1)
        full = product(
            got[:, :LANES],
            jnp.concatenate([held, got[:, LANES:]], axis=1),
            ((0,), (0,)),
        )

        def part(kind, start, size):
            return full[kind * piece : (kind + 1) * piece, start : start + size]

        at_query = features
        at_context = at_query + local_width
        at_d_query = at_context + local_width
        at_d_context = at_d_query + local_width
        grad_projector = -part(0, 0, features).T
        grad_attn_out = part(0, at_context, local_width).T
        grad_query = part(1, at_d_query, local_width)
        grad_key = part(2, at_query, local_width)
        grad_value = part(2 + heads_here, at_d_context, local_width)
        for h in range(1, heads_here):
            here = lane_head == h
            grad_key = jnp.where(here, part(2 + h, at_query, local_width), grad_key)
            grad_value = jnp.where(
                here, part(2 + heads_here + h, at_d_context, local_width), grad_value
            )
        return (jnp.stack([grad_query, grad_key, grad_value]), grad_attn_out, grad_projector)

    return local


def solution(mesh):
    placed = (
        P("wide", "narrow"),
        P("narrow"),
        P("narrow", "wide"),
        P("wide", "narrow"),
        P("narrow", "wide"),
        P("wide", None, None),
        P("wide", None),
        P(None, None, "narrow"),
        P("narrow", None),
    )
    return jax.shard_map(
        make_local(mesh.shape["wide"], mesh.shape["narrow"], Z_PARTS, CORES),
        mesh=mesh,
        in_specs=placed,
        out_specs=(P(None, "wide", "narrow"), P("narrow", "wide"), P("narrow", "wide")),
        check_vma=False,
    )
```

```python
import jax
import jax.numpy as jnp
from jax import lax
from jax.sharding import PartitionSpec as P

HEAD_DIM = 64
LANES = 128
EPSILON = 1e-06
CORES = 2

f32 = jnp.float32
bf16 = jnp.bfloat16


def product(left, right, dims=((1,), (0,))):
    return lax.dot_general(left, right, (dims, ((), ())), preferred_element_type=f32)


def chip_groups(wide, cores):
    return [[chip * cores + c for chip in range(wide // cores)] for c in range(cores)]


def exchange(block, axis, groups=None):
    return lax.all_to_all(block, axis, 0, 0, axis_index_groups=groups)


def spread(block, axis, count, groups=None):
    return exchange(jnp.broadcast_to(block[None], (count,) + block.shape), axis, groups)


def make_local(wide, narrow):
    chips = wide // CORES
    groups = chip_groups(wide, CORES)
    pairs = [(i, i ^ 1) for i in range(wide)]

    def swap(block):
        return lax.ppermute(block, "wide", pairs)

    def local(
        teacher_in,
        teacher_gain,
        mlp_in,
        mlp_out,
        projector,
        student_in,
        sample_pos,
        w_qkv,
        w_attn_out,
    ):
        rows, features = teacher_in.shape
        d_t = features * narrow
        images, patches, width = student_in.shape
        select = sample_pos.shape[1]
        local_width = w_qkv.shape[2]
        scale = HEAD_DIM ** (-0.5)
        half = rows * chips
        first_core = lax.axis_index("wide") % CORES == 0

        own = teacher_in.astype(f32)
        sums = jnp.concatenate(
            [
                jnp.sum(own, axis=1, keepdims=True),
                jnp.sum(own * own, axis=1, keepdims=True),
            ],
            axis=1,
        )
        sums = jnp.sum(spread(sums, "narrow", narrow), axis=0)
        center = sums[:, 0:1] / d_t
        variance = sums[:, 1:2] / d_t - center * center
        normed = (
            (own - center) * lax.rsqrt(variance + EPSILON) * teacher_gain.astype(f32)
        ).astype(bf16)
        normed = spread(normed, "wide", chips, groups).reshape(half, features)
        normed_other = swap(normed)

        pre = jnp.concatenate(
            [
                product(block, mlp_in).astype(bf16).reshape(narrow, half // narrow, -1)
                for block in (normed, normed_other)
            ],
            axis=1,
        )
        pre = jnp.sum(exchange(pre, "narrow").astype(f32), axis=0)
        hidden = jax.nn.gelu(pre, approximate=False).astype(bf16)
        hidden = spread(hidden, "narrow", narrow)
        hidden_own = hidden[:, : half // narrow].reshape(half, -1)
        hidden_other = hidden[:, half // narrow :].reshape(half, -1)
        branch = swap(product(hidden_other, mlp_out).astype(bf16))
        branch = (product(hidden_own, mlp_out) + branch.astype(f32)).astype(bf16)
        branch = exchange(branch.reshape(chips, rows, features), "wide", groups)
        teacher_local = (own + jnp.sum(branch.astype(f32), axis=0)).astype(bf16)

        columns = spread(projector.T, "wide", chips, groups)
        columns_other = swap(columns)
        columns = jnp.stack(
            [
                jnp.where(first_core, columns, columns_other),
                jnp.where(first_core, columns_other, columns),
            ],
            axis=1,
        ).reshape(-1, features)

        flat_in = student_in.reshape(images * patches, width)
        source = flat_in.astype(f32)
        center_s = jnp.mean(source, axis=-1, keepdims=True)
        spread_s = jnp.mean(source * source, axis=-1, keepdims=True) - center_s * center_s
        flat_norm = ((source - center_s) * lax.rsqrt(spread_s + EPSILON)).astype(bf16)
        keys = product(flat_norm, w_qkv[1]).astype(bf16)
        values = product(flat_norm, w_qkv[2]).astype(bf16)
        picks = images * select
        column = lax.broadcasted_iota(jnp.int32, (picks, images * patches), 1)
        pick_image = lax.broadcasted_iota(jnp.int32, (picks, 1), 0) // select
        wanted = pick_image * patches + sample_pos.reshape(picks, 1)
        chosen = (column == wanted).astype(bf16)
        picked_norm = product(chosen, flat_norm).astype(bf16)
        picked_in = product(chosen, flat_in)
        queries = product(picked_norm, w_qkv[0]).astype(bf16)
        lane_head = lax.broadcasted_iota(jnp.int32, (1, local_width), 1) // HEAD_DIM
        heads_here = local_width // HEAD_DIM

        def by_head(block):
            return jnp.concatenate(
                [jnp.where(lane_head == h, block, 0).astype(bf16) for h in range(heads_here)]
            )

        def merge_heads(block):
            merged = block[:picks]
            for h in range(1, heads_here):
                merged = jnp.where(lane_head == h, block[h * picks : (h + 1) * picks], merged)
            return merged.astype(bf16)

        scores = product(by_head(queries), keys, ((1,), (1,))) * scale
        own_image = jnp.tile(column // patches == pick_image, (heads_here, 1))
        probs = jax.nn.softmax(jnp.where(own_image, scores, -jnp.inf), axis=-1)
        probs_low = probs.astype(bf16)
        context = merge_heads(product(probs_low, values))
        value_side = product(probs_low, flat_norm).astype(bf16)
        mixed = product(context, w_attn_out)

        target = product(teacher_local, columns, ((1,), (1,)))
        student_out = picked_in + jnp.sum(spread(mixed - target, "narrow", narrow), axis=0)
        delta = (student_out / (select * images)).astype(bf16)

        d_context = product(delta, w_attn_out, ((1,), (1,))).astype(bf16)
        d_probs = product(by_head(d_context), values, ((1,), (1,)))
        d_scores = (
            probs * (d_probs - jnp.sum(probs * d_probs, axis=-1, keepdims=True)) * scale
        ).astype(bf16)
        d_query = merge_heads(product(d_scores, keys))
        key_side = product(d_scores, flat_norm).astype(bf16)

        factors = jnp.concatenate([delta, picked_norm, key_side, value_side], axis=0)
        kinds = factors.shape[0] // rows
        piece = width // wide
        per_tile = LANES // piece
        tiles = width // LANES
        factors = factors.reshape(kinds, rows, tiles, LANES).transpose(2, 1, 0, 3)
        factors = factors.reshape(tiles * rows, kinds * LANES)
        at_in = lax.broadcasted_iota(jnp.int32, (kinds * LANES, per_tile * LANES), 0)
        at_out = lax.broadcasted_iota(jnp.int32, (kinds * LANES, per_tile * LANES), 1)
        lane_in, kind_in = at_in % LANES, at_in // LANES
        lane_out, tile_out = at_out % LANES, at_out // LANES
        move = (
            (lane_in // piece == tile_out)
            & (lane_out // piece == kind_in)
            & (lane_in % piece == lane_out % piece)
        ).astype(bf16)
        packed = product(factors, move).astype(bf16)
        packed = packed.reshape(tiles, rows, per_tile, LANES).transpose(0, 2, 1, 3)
        packed = packed.reshape(chips, CORES, rows, LANES)
        shared = jnp.concatenate([teacher_local, queries, context, d_query, d_context], axis=1)
        shared_width = shared.shape[1]
        shared = jnp.broadcast_to(shared[None], (chips,) + shared.shape)
        got = jnp.concatenate([shared] + [packed[:, c] for c in range(CORES)], axis=2)
        got = exchange(got, "wide", groups).reshape(half, -1)
        got_other = swap(got)

        def rows_product(block):
            ours = jnp.where(
                first_core,
                block[:, shared_width : shared_width + LANES],
                block[:, shared_width + LANES :],
            )
            return product(ours, block[:, :shared_width], ((0,), (0,)))

        full = rows_product(got) + rows_product(got_other)

        def part(kind, start, size):
            return full[kind * piece : (kind + 1) * piece, start : start + size]

        at_query = features
        at_context = at_query + local_width
        at_d_query = at_context + local_width
        at_d_context = at_d_query + local_width
        grad_projector = -part(0, 0, features).T
        grad_attn_out = part(0, at_context, local_width).T
        grad_query = part(1, at_d_query, local_width)
        grad_key = part(2, at_query, local_width)
        grad_value = part(2 + heads_here, at_d_context, local_width)
        for h in range(1, heads_here):
            here = lane_head == h
            grad_key = jnp.where(here, part(2 + h, at_query, local_width), grad_key)
            grad_value = jnp.where(
                here, part(2 + heads_here + h, at_d_context, local_width), grad_value
            )
        return (jnp.stack([grad_query, grad_key, grad_value]), grad_attn_out, grad_projector)

    return local


def solution(mesh):
    placed = (
        P("wide", "narrow"),
        P("narrow"),
        P("narrow", "wide"),
        P("wide", "narrow"),
        P("narrow", "wide"),
        P("wide", None, None),
        P("wide", None),
        P(None, None, "narrow"),
        P("narrow", None),
    )
    return jax.shard_map(
        make_local(mesh.shape["wide"], mesh.shape["narrow"]),
        mesh=mesh,
        in_specs=placed,
        out_specs=(P(None, "wide", "narrow"), P("narrow", "wide"), P("narrow", "wide")),
        check_vma=False,
    )
```

```python
import functools

import jax
import jax.numpy as jnp
import numpy as np
from jax import lax
from jax.experimental import pallas as pl
from jax.experimental.pallas import tpu as pltpu
from jax.sharding import PartitionSpec as P

HEAD_DIM = 64
LANES = 128
EPSILON = 1e-06
CORES = 2

f32 = jnp.float32
bf16 = jnp.bfloat16


def product(left, right, dims=((1,), (0,))):
    return lax.dot_general(left, right, (dims, ((), ())), preferred_element_type=f32)


def chip_groups(wide, cores):
    return [[chip * cores + c for chip in range(wide // cores)] for c in range(cores)]


def exchange(block, axis, groups=None):
    return lax.all_to_all(block, axis, 0, 0, axis_index_groups=groups)


def spread(block, axis, count, groups=None):
    return exchange(jnp.broadcast_to(block[None], (count,) + block.shape), axis, groups)


def by_head(block, heads):
    lane_head = lax.broadcasted_iota(jnp.int32, block.shape, 1) // HEAD_DIM
    return jnp.concatenate([jnp.where(lane_head == h, block, 0.0) for h in range(heads)], axis=0)


def merge_heads(block, heads):
    picks = block.shape[0] // heads
    merged = block[:picks]
    lane_head = lax.broadcasted_iota(jnp.int32, merged.shape, 1) // HEAD_DIM
    for h in range(1, heads):
        merged = jnp.where(lane_head == h, block[h * picks : (h + 1) * picks], merged)
    return merged


def rounded(block):
    return block.astype(bf16).astype(f32)


def forward_kernel(
    patches,
    wanted_ref,
    first_ref,
    student_ref,
    w_qkv_ref,
    w_out_ref,
    norm_ref,
    keys_ref,
    values_ref,
    probs_ref,
    side_ref,
    early_ref,
    picked_norm_ref,
    picked_in_ref,
    mixed_ref,
):
    total, width = student_ref.shape
    heads = keys_ref.shape[1] // HEAD_DIM
    for start in range(0, total, patches):
        at = pl.ds(start, patches)
        source = student_ref[at, :].astype(f32)
        center = jnp.mean(source, axis=1, keepdims=True)
        spread_s = jnp.mean(source * source, axis=1, keepdims=True) - center * center
        norm = ((source - center) * lax.rsqrt(spread_s + EPSILON)).astype(bf16)
        norm_ref[at, :] = norm
        keys_ref[at, :] = product(norm, w_qkv_ref[1]).astype(bf16)
        values_ref[at, :] = product(norm, w_qkv_ref[2]).astype(bf16)
    norm = norm_ref[...]
    picks = wanted_ref.shape[0]
    column = lax.broadcasted_iota(jnp.int32, (picks, total), 1)
    chosen = jnp.where(column == wanted_ref[...], 1.0, 0.0).astype(bf16)
    picked_norm = product(chosen, norm)
    picked_norm_ref[...] = picked_norm
    picked_in_ref[...] = product(chosen, student_ref[...])
    queries = product(picked_norm.astype(bf16), w_qkv_ref[0])
    scores = product(by_head(queries, heads).astype(bf16), keys_ref[...], ((1,), (1,)))
    column = lax.broadcasted_iota(jnp.int32, scores.shape, 1)
    first = first_ref[...]
    inside = (column >= first) & (column < first + patches)
    scores = jnp.where(inside, scores * HEAD_DIM ** (-0.5), -jnp.inf)
    top = jnp.max(scores, axis=1, keepdims=True)
    powers = jnp.where(inside, jnp.exp(scores - top), 0.0)
    probs = powers / jnp.sum(powers, axis=1, keepdims=True)
    probs_ref[...] = probs
    probs_low = probs.astype(bf16)
    context = merge_heads(product(probs_low, values_ref[...]), heads)
    side_ref[...] = product(probs_low, norm)
    early_ref[...] = jnp.concatenate([queries, context], axis=1)
    mixed_ref[...] = product(context.astype(bf16), w_out_ref[...])


def backward_kernel(
    divisor,
    terms_ref,
    picked_in_ref,
    probs_ref,
    keys_ref,
    values_ref,
    norm_ref,
    w_out_ref,
    picked_norm_ref,
    side_ref,
    early_ref,
    teacher_ref,
    move_ref,
    send_ref,
):
    picks, width = picked_in_ref.shape
    local_width = keys_ref.shape[1]
    heads = local_width // HEAD_DIM
    delta = (picked_in_ref[...] + jnp.sum(terms_ref[...], axis=0)) / divisor
    d_context = product(delta.astype(bf16), w_out_ref[...], ((1,), (1,)))
    d_probs = product(by_head(d_context, heads).astype(bf16), values_ref[...], ((1,), (1,)))
    probs = probs_ref[...]
    held = jnp.sum(probs * d_probs, axis=1, keepdims=True)
    d_scores = (probs * (d_probs - held) * HEAD_DIM ** (-0.5)).astype(bf16)
    d_query = merge_heads(product(d_scores, keys_ref[...]), heads)
    key_side = product(d_scores, norm_ref[...])
    shared = jnp.concatenate(
        [teacher_ref[...].astype(f32), early_ref[...], d_query, d_context], axis=1
    )
    shared_width = shared.shape[1]
    twice = jnp.concatenate([shared, shared], axis=0).astype(bf16)
    for start in range(0, send_ref.shape[0], 2 * picks):
        send_ref[pl.ds(start, 2 * picks), pl.ds(0, shared_width)] = twice

    side = side_ref[...]
    factors = [delta, picked_norm_ref[...]]
    factors += [key_side[h * picks : (h + 1) * picks] for h in range(heads)]
    factors += [side[h * picks : (h + 1) * picks] for h in range(heads)]
    lines = [
        jnp.concatenate([factor[:, at : at + LANES] for factor in factors], axis=1)
        for at in range(0, width, LANES)
    ]
    packed = product(jnp.concatenate(lines, axis=0).astype(bf16), move_ref[...])
    per_tile = packed.shape[1] // LANES
    chips_per_tile = per_tile // CORES
    for chip in range(0, send_ref.shape[0] // picks, 2):
        tile, place = chip // chips_per_tile, chip % chips_per_tile
        for core in range(CORES):
            pieces = []
            for spot in (place, place + 1):
                lane = (spot * CORES + core) * LANES
                pieces.append(packed[tile * picks : (tile + 1) * picks, lane : lane + LANES])
            send_ref[
                pl.ds(chip * picks, 2 * picks), pl.ds(shared_width + core * LANES, LANES)
            ] = jnp.concatenate(pieces, axis=0).astype(bf16)


def call_kernel(kernel, out_shape, flops, *operands):
    whole = pl.BlockSpec(memory_space=pltpu.VMEM)
    moved = sum(x.size * x.dtype.itemsize for x in operands)
    return pl.pallas_call(
        kernel,
        out_shape=out_shape,
        in_specs=[whole] * len(operands),
        out_specs=jax.tree.map(lambda _: whole, out_shape),
        compiler_params=pltpu.CompilerParams(vmem_limit_bytes=40 * 2**20),
        cost_estimate=pl.CostEstimate(flops=flops, bytes_accessed=moved, transcendentals=0),
    )(*operands)


def lane_moves(kinds, piece):
    per_tile = LANES // piece
    move = np.zeros((kinds, LANES, per_tile, LANES), np.float32)
    for kind in range(kinds):
        for tile in range(per_tile):
            for lane in range(piece):
                move[kind, tile * piece + lane, tile, kind * piece + lane] = 1.0
    return move.reshape(kinds * LANES, per_tile * LANES)


def make_local(wide, narrow):
    chips = wide // CORES
    groups = chip_groups(wide, CORES)
    pairs = [(i, i ^ 1) for i in range(wide)]

    def swap(block):
        return lax.ppermute(block, "wide", pairs)

    def doubled(blocks, bit):
        other = lax.ppermute(blocks, "wide", [(i, i ^ bit) for i in range(wide)])
        mine = (lax.axis_index("wide") & bit != 0).astype(jnp.int32)
        place = lax.broadcasted_iota(jnp.int32, (1, 2) + blocks.shape[1:], 1)
        both = jnp.where(place == mine, blocks[:, None], other[:, None])
        return both.reshape((-1,) + blocks.shape[1:])

    bits = []
    while 2 ** len(bits) < wide:
        bits.insert(0, 2 ** len(bits))

    def local(
        teacher_in,
        teacher_gain,
        mlp_in,
        mlp_out,
        projector,
        student_in,
        sample_pos,
        w_qkv,
        w_attn_out,
    ):
        rows, features = teacher_in.shape
        d_t = features * narrow
        images, patches, width = student_in.shape
        select = sample_pos.shape[1]
        local_width = w_qkv.shape[2]
        half = rows * chips
        first_core = lax.axis_index("wide") % CORES == 0
        heads_here = local_width // HEAD_DIM
        picks = images * select

        image_first = np.repeat(np.arange(images, dtype=np.int32) * patches, select)[:, None]
        flat_in = student_in.reshape(images * patches, width)
        norm_shape = jax.ShapeDtypeStruct(flat_in.shape, bf16)
        head_shape = jax.ShapeDtypeStruct((flat_in.shape[0], local_width), bf16)
        score_shape = jax.ShapeDtypeStruct((heads_here * picks, flat_in.shape[0]), f32)
        side_shape = jax.ShapeDtypeStruct((heads_here * picks, width), f32)
        early_shape = jax.ShapeDtypeStruct((picks, 2 * local_width), f32)
        row_shape = jax.ShapeDtypeStruct((picks, width), f32)
        student = call_kernel(
            functools.partial(forward_kernel, patches),
            [norm_shape, head_shape, head_shape, score_shape, side_shape, early_shape]
            + [row_shape] * 3,
            2 * flat_in.size * (2 * local_width + 4 * picks),
            sample_pos.reshape(picks, 1) + image_first,
            jnp.asarray(np.tile(image_first, (heads_here, 1))),
            flat_in,
            w_qkv,
            w_attn_out,
        )

        own = teacher_in.astype(f32)
        sums = jnp.concatenate(
            [
                jnp.sum(own, axis=1, keepdims=True),
                jnp.sum(own * own, axis=1, keepdims=True),
            ],
            axis=1,
        )
        sums = jnp.sum(spread(sums, "narrow", narrow), axis=0)
        center = sums[:, 0:1] / d_t
        variance = sums[:, 1:2] / d_t - center * center
        normed = (
            (own - center) * lax.rsqrt(variance + EPSILON) * teacher_gain.astype(f32)
        ).astype(bf16)
        normed = spread(normed, "wide", chips, groups).reshape(half, features)
        columns = projector.T[None]
        for bit in bits[:-3]:
            columns = doubled(columns, bit)
        normed, columns, student = lax.optimization_barrier((normed, columns, student))
        norm, keys, values, probs, side, early, picked_norm, picked_in, mixed = student
        normed_other = swap(normed)

        pre = jnp.concatenate(
            [
                product(block, mlp_in).astype(bf16).reshape(narrow, half // narrow, -1)
                for block in (normed, normed_other)
            ],
            axis=1,
        )
        pre = exchange(pre, "narrow")
        columns = doubled(columns, bits[-3])
        pre, columns = lax.optimization_barrier((pre, columns))
        pre = jnp.sum(pre.astype(f32), axis=0)
        hidden = jax.nn.gelu(pre, approximate=False).astype(bf16)
        hidden = spread(hidden, "narrow", narrow)
        columns = doubled(columns, bits[-2])
        hidden, columns = lax.optimization_barrier((hidden, columns))
        hidden_own = hidden[:, : half // narrow].reshape(half, -1)
        hidden_other = hidden[:, half // narrow :].reshape(half, -1)
        branch = swap(product(hidden_other, mlp_out).astype(bf16))
        branch = (product(hidden_own, mlp_out) + branch.astype(f32)).astype(bf16)
        branch = exchange(branch.reshape(chips, rows, features), "wide", groups)
        teacher_local = (own + jnp.sum(branch.astype(f32), axis=0)).astype(bf16)

        columns = doubled(columns, bits[-1]).reshape(-1, features)
        target = product(teacher_local, columns, ((1,), (1,)))
        terms = spread(mixed - target, "narrow", narrow)

        piece = width // wide
        kinds = 2 + 2 * heads_here
        shared_width = features + 4 * local_width
        got = call_kernel(
            functools.partial(backward_kernel, float(select * images)),
            jax.ShapeDtypeStruct((half, shared_width + CORES * LANES), bf16),
            2 * norm.size * heads_here * picks,
            terms,
            picked_in,
            probs,
            keys,
            values,
            norm,
            w_attn_out,
            picked_norm,
            side,
            early,
            teacher_local,
            jnp.asarray(lane_moves(kinds, piece), bf16),
        )
        got = exchange(got.reshape(chips, rows, -1), "wide", groups).reshape(half, -1)
        got_other = swap(got)

        def rows_product(block):
            ours = jnp.where(
                first_core,
                block[:, shared_width : shared_width + LANES],
                block[:, shared_width + LANES :],
            )
            return product(ours, block[:, :shared_width], ((0,), (0,)))

        full = rows_product(got) + rows_product(got_other)

        def part(kind, start, size):
            return full[kind * piece : (kind + 1) * piece, start : start + size]

        at_query = features
        at_context = at_query + local_width
        at_d_query = at_context + local_width
        at_d_context = at_d_query + local_width
        grad_projector = -part(0, 0, features).T
        grad_attn_out = part(0, at_context, local_width).T
        grad_query = part(1, at_d_query, local_width)
        grad_key = part(2, at_query, local_width)
        grad_value = part(2 + heads_here, at_d_context, local_width)
        for h in range(1, heads_here):
            here = lax.broadcasted_iota(jnp.int32, grad_key.shape, 1) // HEAD_DIM == h
            grad_key = jnp.where(here, part(2 + h, at_query, local_width), grad_key)
            grad_value = jnp.where(
                here, part(2 + heads_here + h, at_d_context, local_width), grad_value
            )
        return (jnp.stack([grad_query, grad_key, grad_value]), grad_attn_out, grad_projector)

    return local


def solution(mesh):
    placed = (
        P("wide", "narrow"),
        P("narrow"),
        P("narrow", "wide"),
        P("wide", "narrow"),
        P("narrow", "wide"),
        P("wide", None, None),
        P("wide", None),
        P(None, None, "narrow"),
        P("narrow", None),
    )
    return jax.shard_map(
        make_local(mesh.shape["wide"], mesh.shape["narrow"]),
        mesh=mesh,
        in_specs=placed,
        out_specs=(P(None, "wide", "narrow"), P("narrow", "wide"), P("narrow", "wide")),
        check_vma=False,
    )
```

```python
import functools

import jax
import jax.numpy as jnp
import numpy as np
from jax import lax
from jax.experimental import pallas as pl
from jax.experimental.pallas import tpu as pltpu
from jax.sharding import PartitionSpec as P

HEAD_DIM = 64
LANES = 128
EPSILON = 1e-06
CORES = 2

f32 = jnp.float32
bf16 = jnp.bfloat16


def product(left, right, dims=((1,), (0,))):
    return lax.dot_general(left, right, (dims, ((), ())), preferred_element_type=f32)


def chip_groups(wide, cores):
    return [[chip * cores + c for chip in range(wide // cores)] for c in range(cores)]


def exchange(block, axis, groups=None):
    return lax.all_to_all(block, axis, 0, 0, axis_index_groups=groups)


def spread(block, axis, count, groups=None):
    return exchange(jnp.broadcast_to(block[None], (count,) + block.shape), axis, groups)


def by_head(block, heads):
    lane_head = lax.broadcasted_iota(jnp.int32, block.shape, 1) // HEAD_DIM
    return jnp.concatenate([jnp.where(lane_head == h, block, 0.0) for h in range(heads)], axis=0)


def merge_heads(block, heads):
    picks = block.shape[0] // heads
    merged = block[:picks]
    lane_head = lax.broadcasted_iota(jnp.int32, merged.shape, 1) // HEAD_DIM
    for h in range(1, heads):
        merged = jnp.where(lane_head == h, block[h * picks : (h + 1) * picks], merged)
    return merged


def rounded(block):
    return block.astype(bf16).astype(f32)


def forward_kernel(
    patches,
    wanted_ref,
    first_ref,
    student_ref,
    w_qkv_ref,
    w_out_ref,
    norm_ref,
    keys_ref,
    values_ref,
    probs_ref,
    side_ref,
    early_ref,
    picked_norm_ref,
    picked_in_ref,
    mixed_ref,
):
    total, width = student_ref.shape
    heads = keys_ref.shape[1] // HEAD_DIM
    for start in range(0, total, patches):
        at = pl.ds(start, patches)
        source = student_ref[at, :].astype(f32)
        center = jnp.mean(source, axis=1, keepdims=True)
        spread_s = jnp.mean(source * source, axis=1, keepdims=True) - center * center
        norm = ((source - center) * lax.rsqrt(spread_s + EPSILON)).astype(bf16)
        norm_ref[at, :] = norm
        keys_ref[at, :] = product(norm, w_qkv_ref[1]).astype(bf16)
        values_ref[at, :] = product(norm, w_qkv_ref[2]).astype(bf16)
    norm = norm_ref[...]
    picks = wanted_ref.shape[0]
    column = lax.broadcasted_iota(jnp.int32, (picks, total), 1)
    chosen = jnp.where(column == wanted_ref[...], 1.0, 0.0).astype(bf16)
    picked_norm = product(chosen, norm)
    picked_norm_ref[...] = picked_norm
    picked_in_ref[...] = product(chosen, student_ref[...])
    queries = product(picked_norm.astype(bf16), w_qkv_ref[0])
    scores = product(by_head(queries, heads).astype(bf16), keys_ref[...], ((1,), (1,)))
    column = lax.broadcasted_iota(jnp.int32, scores.shape, 1)
    first = first_ref[...]
    inside = (column >= first) & (column < first + patches)
    scores = jnp.where(inside, scores * HEAD_DIM ** (-0.5), -jnp.inf)
    top = jnp.max(scores, axis=1, keepdims=True)
    powers = jnp.where(inside, jnp.exp(scores - top), 0.0)
    probs = powers / jnp.sum(powers, axis=1, keepdims=True)
    probs_ref[...] = probs
    probs_low = probs.astype(bf16)
    context = merge_heads(product(probs_low, values_ref[...]), heads)
    side_ref[...] = product(probs_low, norm)
    early_ref[...] = jnp.concatenate([queries, context], axis=1)
    mixed_ref[...] = product(context.astype(bf16), w_out_ref[...])


def backward_kernel(
    divisor,
    terms_ref,
    picked_in_ref,
    probs_ref,
    keys_ref,
    values_ref,
    norm_ref,
    w_out_ref,
    picked_norm_ref,
    side_ref,
    early_ref,
    teacher_ref,
    move_ref,
    send_ref,
):
    picks, width = picked_in_ref.shape
    local_width = keys_ref.shape[1]
    heads = local_width // HEAD_DIM
    delta = (picked_in_ref[...] + jnp.sum(terms_ref[...], axis=0)) / divisor
    d_context = product(delta.astype(bf16), w_out_ref[...], ((1,), (1,)))
    d_probs = product(by_head(d_context, heads).astype(bf16), values_ref[...], ((1,), (1,)))
    probs = probs_ref[...]
    held = jnp.sum(probs * d_probs, axis=1, keepdims=True)
    d_scores = (probs * (d_probs - held) * HEAD_DIM ** (-0.5)).astype(bf16)
    d_query = merge_heads(product(d_scores, keys_ref[...]), heads)
    key_side = product(d_scores, norm_ref[...])
    shared = jnp.concatenate(
        [teacher_ref[...].astype(f32), early_ref[...], d_query, d_context], axis=1
    )
    shared_width = shared.shape[1]
    twice = jnp.concatenate([shared, shared], axis=0).astype(bf16)
    for start in range(0, send_ref.shape[0], 2 * picks):
        send_ref[pl.ds(start, 2 * picks), pl.ds(0, shared_width)] = twice

    side = side_ref[...]
    factors = [delta, picked_norm_ref[...]]
    factors += [key_side[h * picks : (h + 1) * picks] for h in range(heads)]
    factors += [side[h * picks : (h + 1) * picks] for h in range(heads)]
    lines = [
        jnp.concatenate([factor[:, at : at + LANES] for factor in factors], axis=1)
        for at in range(0, width, LANES)
    ]
    packed = product(jnp.concatenate(lines, axis=0).astype(bf16), move_ref[...])
    per_tile = packed.shape[1] // LANES
    chips_per_tile = per_tile // CORES
    for chip in range(0, send_ref.shape[0] // picks, 2):
        tile, place = chip // chips_per_tile, chip % chips_per_tile
        for core in range(CORES):
            pieces = []
            for spot in (place, place + 1):
                lane = (spot * CORES + core) * LANES
                pieces.append(packed[tile * picks : (tile + 1) * picks, lane : lane + LANES])
            send_ref[
                pl.ds(chip * picks, 2 * picks), pl.ds(shared_width + core * LANES, LANES)
            ] = jnp.concatenate(pieces, axis=0).astype(bf16)


def up_kernel(own_ref, other_ref, weight_ref, send_ref):
    count = own_ref.shape[0] * 2 // send_ref.shape[1]
    size = send_ref.shape[1] // 2
    for place, rows_ref in enumerate((own_ref, other_ref)):
        part = product(rows_ref[...], weight_ref[...]).astype(bf16)
        for n in range(count):
            send_ref[n, pl.ds(place * size, size), :] = part[n * size : (n + 1) * size]


def gelu_kernel(parts_ref, send_ref):
    pre = parts_ref[0].astype(f32)
    for n in range(1, parts_ref.shape[0]):
        pre = pre + parts_ref[n].astype(f32)
    hidden = (0.5 * pre * (1.0 + lax.erf(pre * 0.5**0.5))).astype(bf16)
    for n in range(send_ref.shape[0]):
        send_ref[n] = hidden


def hidden_half(hidden_ref, place):
    size = hidden_ref.shape[1] // 2
    parts = [hidden_ref[n, pl.ds(place * size, size), :] for n in range(hidden_ref.shape[0])]
    return jnp.concatenate(parts, axis=0)


def down_other_kernel(hidden_ref, weight_ref, out_ref):
    out_ref[...] = product(hidden_half(hidden_ref, 1), weight_ref[...]).astype(bf16)


def down_own_kernel(hidden_ref, weight_ref, add_ref, out_ref):
    own = product(hidden_half(hidden_ref, 0), weight_ref[...])
    out_ref[...] = (own + add_ref[...].astype(f32)).astype(bf16)


def target_kernel(branch_ref, teacher_ref, columns_ref, mixed_ref, local_ref, terms_ref):
    teacher = teacher_ref[...].astype(f32) + jnp.sum(branch_ref[...].astype(f32), axis=0)
    teacher = teacher.astype(bf16)
    local_ref[...] = teacher
    term = mixed_ref[...] - product(teacher, columns_ref[...], ((1,), (1,)))
    for n in range(terms_ref.shape[0]):
        terms_ref[n] = term


def call_kernel(kernel, out_shape, flops, *operands):
    whole = pl.BlockSpec(memory_space=pltpu.VMEM)
    moved = sum(x.size * x.dtype.itemsize for x in operands)
    return pl.pallas_call(
        kernel,
        out_shape=out_shape,
        in_specs=[whole] * len(operands),
        out_specs=jax.tree.map(lambda _: whole, out_shape),
        compiler_params=pltpu.CompilerParams(vmem_limit_bytes=40 * 2**20),
        cost_estimate=pl.CostEstimate(flops=flops, bytes_accessed=moved, transcendentals=0),
    )(*operands)


def lane_moves(kinds, piece):
    per_tile = LANES // piece
    move = np.zeros((kinds, LANES, per_tile, LANES), np.float32)
    for kind in range(kinds):
        for tile in range(per_tile):
            for lane in range(piece):
                move[kind, tile * piece + lane, tile, kind * piece + lane] = 1.0
    return move.reshape(kinds * LANES, per_tile * LANES)


def make_local(wide, narrow):
    chips = wide // CORES
    groups = chip_groups(wide, CORES)
    pairs = [(i, i ^ 1) for i in range(wide)]

    def swap(block):
        return lax.ppermute(block, "wide", pairs)

    def doubled(blocks, bit):
        other = lax.ppermute(blocks, "wide", [(i, i ^ bit) for i in range(wide)])
        mine = (lax.axis_index("wide") & bit != 0).astype(jnp.int32)
        place = lax.broadcasted_iota(jnp.int32, (1, 2) + blocks.shape[1:], 1)
        both = jnp.where(place == mine, blocks[:, None], other[:, None])
        return both.reshape((-1,) + blocks.shape[1:])

    def local(
        teacher_in,
        teacher_gain,
        mlp_in,
        mlp_out,
        projector,
        student_in,
        sample_pos,
        w_qkv,
        w_attn_out,
    ):
        rows, features = teacher_in.shape
        d_t = features * narrow
        images, patches, width = student_in.shape
        select = sample_pos.shape[1]
        local_width = w_qkv.shape[2]
        half = rows * chips
        first_core = lax.axis_index("wide") % CORES == 0
        heads_here = local_width // HEAD_DIM
        picks = images * select

        image_first = np.repeat(np.arange(images, dtype=np.int32) * patches, select)[:, None]
        flat_in = student_in.reshape(images * patches, width)
        norm_shape = jax.ShapeDtypeStruct(flat_in.shape, bf16)
        head_shape = jax.ShapeDtypeStruct((flat_in.shape[0], local_width), bf16)
        score_shape = jax.ShapeDtypeStruct((heads_here * picks, flat_in.shape[0]), f32)
        side_shape = jax.ShapeDtypeStruct((heads_here * picks, width), f32)
        early_shape = jax.ShapeDtypeStruct((picks, 2 * local_width), f32)
        row_shape = jax.ShapeDtypeStruct((picks, width), f32)
        student = call_kernel(
            functools.partial(forward_kernel, patches),
            [norm_shape, head_shape, head_shape, score_shape, side_shape, early_shape]
            + [row_shape] * 3,
            2 * flat_in.size * (2 * local_width + 4 * picks),
            sample_pos.reshape(picks, 1) + image_first,
            jnp.asarray(np.tile(image_first, (heads_here, 1))),
            flat_in,
            w_qkv,
            w_attn_out,
        )

        own = teacher_in.astype(f32)
        sums = jnp.concatenate(
            [
                jnp.sum(own, axis=1, keepdims=True),
                jnp.sum(own * own, axis=1, keepdims=True),
            ],
            axis=1,
        )
        sums = jnp.sum(spread(sums, "narrow", narrow), axis=0)
        center = sums[:, 0:1] / d_t
        variance = sums[:, 1:2] / d_t - center * center
        normed = (
            (own - center) * lax.rsqrt(variance + EPSILON) * teacher_gain.astype(f32)
        ).astype(bf16)
        first = jnp.concatenate([normed, projector.T], axis=0)
        first = spread(first, "wide", chips, groups)
        first, student = lax.optimization_barrier((first, student))
        norm, keys, values, probs, side, early, picked_norm, picked_in, mixed = student
        normed = first[:, :rows].reshape(half, features)
        normed_other = swap(normed)

        hidden_shape = jax.ShapeDtypeStruct((narrow, 2 * half // narrow, mlp_in.shape[1]), bf16)
        rows_shape = jax.ShapeDtypeStruct((half, features), bf16)
        up_flops = 4 * half * mlp_in.size
        pre = call_kernel(up_kernel, hidden_shape, up_flops, normed, normed_other, mlp_in)
        columns = doubled(first[:, rows:], 1).reshape(-1, features)
        pre = exchange(pre, "narrow")
        hidden = exchange(call_kernel(gelu_kernel, hidden_shape, 8 * pre.size, pre), "narrow")
        hidden, columns = lax.optimization_barrier((hidden, columns))
        branch = swap(call_kernel(down_other_kernel, rows_shape, up_flops // 2, hidden, mlp_out))
        branch = call_kernel(
            down_own_kernel, rows_shape, up_flops // 2, hidden, mlp_out, branch
        )
        branch = exchange(branch.reshape(chips, rows, features), "wide", groups)
        teacher_local, terms = call_kernel(
            target_kernel,
            [
                jax.ShapeDtypeStruct((rows, features), bf16),
                jax.ShapeDtypeStruct((narrow, picks, width), f32),
            ],
            2 * rows * columns.size,
            branch,
            teacher_in,
            columns,
            mixed,
        )
        terms = exchange(terms, "narrow")

        piece = width // wide
        kinds = 2 + 2 * heads_here
        shared_width = features + 4 * local_width
        got = call_kernel(
            functools.partial(backward_kernel, float(select * images)),
            jax.ShapeDtypeStruct((half, shared_width + CORES * LANES), bf16),
            2 * norm.size * heads_here * picks,
            terms,
            picked_in,
            probs,
            keys,
            values,
            norm,
            w_attn_out,
            picked_norm,
            side,
            early,
            teacher_local,
            jnp.asarray(lane_moves(kinds, piece), bf16),
        )
        got = exchange(got.reshape(chips, rows, -1), "wide", groups).reshape(half, -1)
        got_other = swap(got)

        def rows_product(block):
            ours = jnp.where(
                first_core,
                block[:, shared_width : shared_width + LANES],
                block[:, shared_width + LANES :],
            )
            return product(ours, block[:, :shared_width], ((0,), (0,)))

        full = rows_product(got) + rows_product(got_other)

        def part(kind, start, size):
            return full[kind * piece : (kind + 1) * piece, start : start + size]

        at_query = features
        at_context = at_query + local_width
        at_d_query = at_context + local_width
        at_d_context = at_d_query + local_width
        grad_projector = -part(0, 0, features).T
        grad_attn_out = part(0, at_context, local_width).T
        grad_query = part(1, at_d_query, local_width)
        grad_key = part(2, at_query, local_width)
        grad_value = part(2 + heads_here, at_d_context, local_width)
        for h in range(1, heads_here):
            here = lax.broadcasted_iota(jnp.int32, grad_key.shape, 1) // HEAD_DIM == h
            grad_key = jnp.where(here, part(2 + h, at_query, local_width), grad_key)
            grad_value = jnp.where(
                here, part(2 + heads_here + h, at_d_context, local_width), grad_value
            )
        return (jnp.stack([grad_query, grad_key, grad_value]), grad_attn_out, grad_projector)

    return local


def solution(mesh):
    placed = (
        P("wide", "narrow"),
        P("narrow"),
        P("narrow", "wide"),
        P("wide", "narrow"),
        P("narrow", "wide"),
        P("wide", None, None),
        P("wide", None),
        P(None, None, "narrow"),
        P("narrow", None),
    )
    return jax.shard_map(
        make_local(mesh.shape["wide"], mesh.shape["narrow"]),
        mesh=mesh,
        in_specs=placed,
        out_specs=(P(None, "wide", "narrow"), P("narrow", "wide"), P("narrow", "wide")),
        check_vma=False,
    )
```

```python
import functools

import jax
import jax.numpy as jnp
import numpy as np
from jax import lax
from jax.experimental import pallas as pl
from jax.experimental.pallas import tpu as pltpu
from jax.sharding import PartitionSpec as P

HEAD_DIM = 64
LANES = 128
EPSILON = 1e-06
CORES = 2

f32 = jnp.float32
bf16 = jnp.bfloat16


def product(left, right, dims=((1,), (0,))):
    return lax.dot_general(left, right, (dims, ((), ())), preferred_element_type=f32)


def chip_groups(wide, cores):
    return [[chip * cores + c for chip in range(wide // cores)] for c in range(cores)]


def exchange(block, axis, groups=None):
    return lax.all_to_all(block, axis, 0, 0, axis_index_groups=groups)


def spread(block, axis, count, groups=None):
    return exchange(jnp.broadcast_to(block[None], (count,) + block.shape), axis, groups)


def by_head(block, heads):
    lane_head = lax.broadcasted_iota(jnp.int32, block.shape, 1) // HEAD_DIM
    return jnp.concatenate([jnp.where(lane_head == h, block, 0.0) for h in range(heads)], axis=0)


def merge_heads(block, heads):
    picks = block.shape[0] // heads
    merged = block[:picks]
    lane_head = lax.broadcasted_iota(jnp.int32, merged.shape, 1) // HEAD_DIM
    for h in range(1, heads):
        merged = jnp.where(lane_head == h, block[h * picks : (h + 1) * picks], merged)
    return merged


def rounded(block):
    return block.astype(bf16).astype(f32)


def forward_kernel(
    patches,
    wanted_ref,
    first_ref,
    student_ref,
    w_qkv_ref,
    w_out_ref,
    norm_ref,
    keys_ref,
    values_ref,
    probs_ref,
    side_ref,
    early_ref,
    picked_norm_ref,
    picked_in_ref,
    mixed_ref,
):
    total, width = student_ref.shape
    heads = keys_ref.shape[1] // HEAD_DIM
    for start in range(0, total, patches):
        at = pl.ds(start, patches)
        source = student_ref[at, :].astype(f32)
        center = jnp.mean(source, axis=1, keepdims=True)
        spread_s = jnp.mean(source * source, axis=1, keepdims=True) - center * center
        norm = ((source - center) * lax.rsqrt(spread_s + EPSILON)).astype(bf16)
        norm_ref[at, :] = norm
        keys_ref[at, :] = product(norm, w_qkv_ref[1]).astype(bf16)
        values_ref[at, :] = product(norm, w_qkv_ref[2]).astype(bf16)
    norm = norm_ref[...]
    picks = wanted_ref.shape[0]
    column = lax.broadcasted_iota(jnp.int32, (picks, total), 1)
    chosen = jnp.where(column == wanted_ref[...], 1.0, 0.0).astype(bf16)
    picked_norm = product(chosen, norm)
    picked_norm_ref[...] = picked_norm
    picked_in_ref[...] = product(chosen, student_ref[...])
    queries = product(picked_norm.astype(bf16), w_qkv_ref[0])
    scores = product(by_head(queries, heads).astype(bf16), keys_ref[...], ((1,), (1,)))
    column = lax.broadcasted_iota(jnp.int32, scores.shape, 1)
    first = first_ref[...]
    inside = (column >= first) & (column < first + patches)
    scores = jnp.where(inside, scores * HEAD_DIM ** (-0.5), -jnp.inf)
    top = jnp.max(scores, axis=1, keepdims=True)
    powers = jnp.where(inside, jnp.exp(scores - top), 0.0)
    probs = powers / jnp.sum(powers, axis=1, keepdims=True)
    probs_ref[...] = probs
    probs_low = probs.astype(bf16)
    context = merge_heads(product(probs_low, values_ref[...]), heads)
    side_ref[...] = product(probs_low, norm)
    early_ref[...] = jnp.concatenate([queries, context], axis=1)
    mixed_ref[...] = product(context.astype(bf16), w_out_ref[...])


def backward_kernel(
    divisor,
    terms_ref,
    picked_in_ref,
    probs_ref,
    keys_ref,
    values_ref,
    norm_ref,
    w_out_ref,
    picked_norm_ref,
    side_ref,
    early_ref,
    teacher_ref,
    move_ref,
    send_ref,
):
    picks, width = picked_in_ref.shape
    local_width = keys_ref.shape[1]
    heads = local_width // HEAD_DIM
    delta = (picked_in_ref[...] + jnp.sum(terms_ref[...].astype(f32), axis=0)) / divisor
    d_context = product(delta.astype(bf16), w_out_ref[...], ((1,), (1,)))
    d_probs = product(by_head(d_context, heads).astype(bf16), values_ref[...], ((1,), (1,)))
    probs = probs_ref[...]
    held = jnp.sum(probs * d_probs, axis=1, keepdims=True)
    d_scores = (probs * (d_probs - held) * HEAD_DIM ** (-0.5)).astype(bf16)
    d_query = merge_heads(product(d_scores, keys_ref[...]), heads)
    key_side = product(d_scores, norm_ref[...])
    shared = jnp.concatenate(
        [teacher_ref[...].astype(f32), early_ref[...], d_query, d_context], axis=1
    )
    shared_width = shared.shape[1]
    twice = jnp.concatenate([shared, shared], axis=0).astype(bf16)
    for start in range(0, send_ref.shape[0], 2 * picks):
        send_ref[pl.ds(start, 2 * picks), pl.ds(0, shared_width)] = twice

    side = side_ref[...]
    factors = [delta, picked_norm_ref[...]]
    factors += [key_side[h * picks : (h + 1) * picks] for h in range(heads)]
    factors += [side[h * picks : (h + 1) * picks] for h in range(heads)]
    lines = [
        jnp.concatenate([factor[:, at : at + LANES] for factor in factors], axis=1)
        for at in range(0, width, LANES)
    ]
    packed = product(jnp.concatenate(lines, axis=0).astype(bf16), move_ref[...])
    per_tile = packed.shape[1] // LANES
    chips_per_tile = per_tile // CORES
    for chip in range(0, send_ref.shape[0] // picks, 2):
        tile, place = chip // chips_per_tile, chip % chips_per_tile
        for core in range(CORES):
            pieces = []
            for spot in (place, place + 1):
                lane = (spot * CORES + core) * LANES
                pieces.append(packed[tile * picks : (tile + 1) * picks, lane : lane + LANES])
            send_ref[
                pl.ds(chip * picks, 2 * picks), pl.ds(shared_width + core * LANES, LANES)
            ] = jnp.concatenate(pieces, axis=0).astype(bf16)


def thirds(block):
    high = rounded(block)
    middle = rounded(block - high)
    return [high, middle, block - high - middle]


def first_kernel(rows_ref, columns_ref, send_ref):
    block = jnp.concatenate([rows_ref[...].astype(f32), columns_ref[...].astype(f32)], axis=0)
    block = block.astype(bf16)
    for n in range(send_ref.shape[0]):
        send_ref[n] = block


def up_kernel(own_ref, other_ref, gain_ref, weight_ref, send_ref):
    parts, _, hidden = send_ref.shape
    size = own_ref.shape[0] // parts
    features = own_ref.shape[1]
    pieces = []
    for n in range(parts):
        pieces += [own_ref[pl.ds(n * size, size), :], other_ref[pl.ds(n * size, size), :]]
    low = jnp.concatenate(pieces, axis=0)
    rows = low.astype(f32)
    gain = gain_ref[...].astype(f32)
    center = jnp.mean(rows, axis=1, keepdims=True)
    pre = product(((rows - center) * gain).astype(bf16), weight_ref[...]).astype(bf16)
    squares = rows * rows
    square_high = squares.astype(bf16)
    square_low = (squares - square_high.astype(f32)).astype(bf16)
    ones = jnp.ones((8, features), bf16)
    flat = ((1,), (1,))
    means = product(ones, low, flat)[0:1] / features
    totals = (product(ones, square_high, flat) + product(ones, square_low, flat))[0:1]
    stats = jnp.concatenate(thirds(means) + thirds(totals), axis=0)
    gains = product(jnp.broadcast_to(gain, (8, features)).astype(bf16), weight_ref[...])[0:1]
    gains = jnp.concatenate(thirds(gains), axis=0)
    span = 2 * size
    for n in range(parts):
        send_ref[n, pl.ds(0, span), :] = pre[n * span : (n + 1) * span]
        tile = n * span // LANES * LANES
        mine = stats[:, tile : tile + LANES]
        if n * span % LANES:
            mine = pltpu.roll(mine, LANES - n * span % LANES, 1)
        lines = [mine] + [jnp.zeros_like(mine)] * (hidden // LANES - 1)
        extra = jnp.concatenate([gains, jnp.concatenate(lines, axis=1)], axis=0)
        extra = jnp.concatenate([extra, jnp.zeros((16 - extra.shape[0], hidden), f32)], axis=0)
        send_ref[n, pl.ds(span, 16), :] = extra.astype(bf16)


def gelu_kernel(d_t, parts_ref, send_ref):
    parts, span, _ = send_ref.shape
    pre = parts_ref[0, pl.ds(0, span), :].astype(f32)
    for n in range(1, parts):
        pre = pre + parts_ref[n, pl.ds(0, span), :].astype(f32)
    extra = [parts_ref[n, pl.ds(span, 16), :].astype(f32) for n in range(parts)]

    def joined(block, at):
        return block[at : at + 1] + block[at + 1 : at + 2] + block[at + 2 : at + 3]

    means = [joined(block, 3)[:, :LANES] for block in extra]
    center = sum(means) / parts
    variance = sum(joined(block, 6)[:, :LANES] for block in extra) / d_t - center * center
    lines = [mean - center for mean in means] + [lax.rsqrt(variance + EPSILON)]
    lines = jnp.concatenate(lines + [jnp.zeros((LANES - parts - 1, LANES), f32)], axis=0)
    lines = lines.T[:span]
    for n in range(parts):
        pre = pre + lines[:, n : n + 1] * joined(extra[n], 0)
    pre = pre * lines[:, parts : parts + 1]
    hidden = (0.5 * pre * (1.0 + lax.erf(pre * 0.5**0.5))).astype(bf16)
    for n in range(parts):
        send_ref[n] = hidden


def hidden_half(hidden_ref, place):
    size = hidden_ref.shape[1] // 2
    parts = [hidden_ref[n, pl.ds(place * size, size), :] for n in range(hidden_ref.shape[0])]
    return jnp.concatenate(parts, axis=0)


def down_other_kernel(hidden_ref, weight_ref, out_ref):
    out_ref[...] = product(hidden_half(hidden_ref, 1), weight_ref[...]).astype(bf16)


def down_own_kernel(hidden_ref, weight_ref, add_ref, out_ref):
    own = product(hidden_half(hidden_ref, 0), weight_ref[...])
    out_ref[...] = (own + add_ref[...].astype(f32)).astype(bf16)


def target_kernel(branch_ref, teacher_ref, columns_ref, mixed_ref, local_ref, terms_ref):
    teacher = teacher_ref[...].astype(f32) + jnp.sum(branch_ref[...].astype(f32), axis=0)
    teacher = teacher.astype(bf16)
    local_ref[...] = teacher
    term = mixed_ref[...] - product(teacher, columns_ref[...], ((1,), (1,)))
    term = term.astype(bf16)
    for n in range(terms_ref.shape[0]):
        terms_ref[n] = term


def partial_kernel(piece, features, local_width, core_ref, got_ref, mine_ref, theirs_ref):
    heads = local_width // HEAD_DIM
    shared_width = got_ref.shape[1] - CORES * LANES
    shared = got_ref[:, :shared_width]
    starts = [features + n * local_width for n in range(4)]
    both = []
    for core in range(CORES):
        factors = got_ref[:, shared_width + core * LANES : shared_width + (core + 1) * LANES]
        full = product(factors, shared, ((0,), (0,)))

        def part(kind, start, size):
            return full[kind * piece : (kind + 1) * piece, start : start + size]

        def per_head(kind, start):
            block = part(kind, start, local_width)
            head = lax.broadcasted_iota(jnp.int32, block.shape, 1) // HEAD_DIM
            for h in range(1, heads):
                block = jnp.where(head == h, part(kind + h, start, local_width), block)
            return block

        both.append(
            jnp.concatenate(
                [
                    -part(0, 0, features),
                    part(0, starts[1], local_width),
                    part(1, starts[2], local_width),
                    per_head(2, starts[0]),
                    per_head(2 + heads, starts[3]),
                ],
                axis=1,
            )
        )
    first = core_ref[...] == 0
    mine_ref[...] = jnp.where(first, both[0], both[1])
    theirs_ref[...] = jnp.where(first, both[1], both[0])


def total_kernel(mine_ref, other_ref, projector_ref, attn_ref, qkv_ref):
    total = mine_ref[...] + other_ref[...]
    features, local_width = projector_ref.shape[1], attn_ref.shape[1]
    projector_ref[...] = total[:, :features]
    attn_ref[...] = total[:, features : features + local_width]
    for n in range(3):
        start = features + (n + 1) * local_width
        qkv_ref[n] = total[:, start : start + local_width]


def call_kernel(kernel, out_shape, flops, *operands):
    whole = pl.BlockSpec(memory_space=pltpu.VMEM)
    moved = sum(x.size * x.dtype.itemsize for x in operands)
    return pl.pallas_call(
        kernel,
        out_shape=out_shape,
        in_specs=[whole] * len(operands),
        out_specs=jax.tree.map(lambda _: whole, out_shape),
        compiler_params=pltpu.CompilerParams(vmem_limit_bytes=40 * 2**20),
        cost_estimate=pl.CostEstimate(flops=flops, bytes_accessed=moved, transcendentals=0),
    )(*operands)


def lane_moves(kinds, piece):
    per_tile = LANES // piece
    move = np.zeros((kinds, LANES, per_tile, LANES), np.float32)
    for kind in range(kinds):
        for tile in range(per_tile):
            for lane in range(piece):
                move[kind, tile * piece + lane, tile, kind * piece + lane] = 1.0
    return move.reshape(kinds * LANES, per_tile * LANES)


def make_local(wide, narrow):
    chips = wide // CORES
    groups = chip_groups(wide, CORES)
    pairs = [(i, i ^ 1) for i in range(wide)]

    def swap(block):
        return lax.ppermute(block, "wide", pairs)

    def doubled(blocks, bit):
        other = lax.ppermute(blocks, "wide", [(i, i ^ bit) for i in range(wide)])
        mine = (lax.axis_index("wide") & bit != 0).astype(jnp.int32)
        place = lax.broadcasted_iota(jnp.int32, (1, 2) + blocks.shape[1:], 1)
        both = jnp.where(place == mine, blocks[:, None], other[:, None])
        return both.reshape((-1,) + blocks.shape[1:])

    def local(
        teacher_in,
        teacher_gain,
        mlp_in,
        mlp_out,
        projector,
        student_in,
        sample_pos,
        w_qkv,
        w_attn_out,
    ):
        rows, features = teacher_in.shape
        d_t = features * narrow
        images, patches, width = student_in.shape
        select = sample_pos.shape[1]
        local_width = w_qkv.shape[2]
        half = rows * chips
        heads_here = local_width // HEAD_DIM
        picks = images * select

        image_first = np.repeat(np.arange(images, dtype=np.int32) * patches, select)[:, None]
        flat_in = student_in.reshape(images * patches, width)
        norm_shape = jax.ShapeDtypeStruct(flat_in.shape, bf16)
        head_shape = jax.ShapeDtypeStruct((flat_in.shape[0], local_width), bf16)
        score_shape = jax.ShapeDtypeStruct((heads_here * picks, flat_in.shape[0]), f32)
        side_shape = jax.ShapeDtypeStruct((heads_here * picks, width), f32)
        early_shape = jax.ShapeDtypeStruct((picks, 2 * local_width), f32)
        row_shape = jax.ShapeDtypeStruct((picks, width), f32)
        student = call_kernel(
            functools.partial(forward_kernel, patches),
            [norm_shape, head_shape, head_shape, score_shape, side_shape, early_shape]
            + [row_shape] * 3,
            2 * flat_in.size * (2 * local_width + 4 * picks),
            sample_pos.reshape(picks, 1) + image_first,
            jnp.asarray(np.tile(image_first, (heads_here, 1))),
            flat_in,
            w_qkv,
            w_attn_out,
        )

        piece = width // wide
        first = call_kernel(
            first_kernel,
            jax.ShapeDtypeStruct((chips, rows + piece, features), bf16),
            chips * (rows + piece) * features,
            teacher_in,
            projector.T,
        )
        first = exchange(first, "wide", groups)
        first, student = lax.optimization_barrier((first, student))
        norm, keys, values, probs, side, early, picked_norm, picked_in, mixed = student
        raw = first[:, :rows].reshape(half, features)
        raw_other = swap(raw)

        hidden_shape = jax.ShapeDtypeStruct((narrow, 2 * half // narrow, mlp_in.shape[1]), bf16)
        rows_shape = jax.ShapeDtypeStruct((half, features), bf16)
        up_flops = 4 * half * mlp_in.size
        pre = call_kernel(
            up_kernel,
            jax.ShapeDtypeStruct((narrow, 2 * half // narrow + 16, mlp_in.shape[1]), bf16),
            up_flops,
            raw,
            raw_other,
            teacher_gain.reshape(1, features),
            mlp_in,
        )
        columns = doubled(first[:, rows:], 1).reshape(-1, features)
        pre = exchange(pre, "narrow")
        hidden = call_kernel(functools.partial(gelu_kernel, d_t), hidden_shape, 8 * pre.size, pre)
        hidden = exchange(hidden, "narrow")
        hidden, columns = lax.optimization_barrier((hidden, columns))
        branch = swap(call_kernel(down_other_kernel, rows_shape, up_flops // 2, hidden, mlp_out))
        branch = call_kernel(
            down_own_kernel, rows_shape, up_flops // 2, hidden, mlp_out, branch
        )
        branch = exchange(branch.reshape(chips, rows, features), "wide", groups)
        teacher_local, terms = call_kernel(
            target_kernel,
            [
                jax.ShapeDtypeStruct((rows, features), bf16),
                jax.ShapeDtypeStruct((narrow, picks, width), bf16),
            ],
            2 * rows * columns.size,
            branch,
            teacher_in,
            columns,
            mixed,
        )
        terms = exchange(terms, "narrow")

        kinds = 2 + 2 * heads_here
        shared_width = features + 4 * local_width
        got = call_kernel(
            functools.partial(backward_kernel, float(select * images)),
            jax.ShapeDtypeStruct((half, shared_width + CORES * LANES), bf16),
            2 * norm.size * heads_here * picks,
            terms,
            picked_in,
            probs,
            keys,
            values,
            norm,
            w_attn_out,
            picked_norm,
            side,
            early,
            teacher_local,
            jnp.asarray(lane_moves(kinds, piece), bf16),
        )
        got = exchange(got.reshape(chips, rows, -1), "wide", groups).reshape(half, -1)
        totals_shape = jax.ShapeDtypeStruct((piece, shared_width), f32)
        mine, theirs = call_kernel(
            functools.partial(partial_kernel, piece, features, local_width),
            [totals_shape, totals_shape],
            4 * LANES * half * shared_width,
            (lax.axis_index("wide") % CORES).reshape(1, 1),
            got,
        )
        grad_projector, grad_attn_out, grad_qkv = call_kernel(
            total_kernel,
            [
                jax.ShapeDtypeStruct((piece, features), f32),
                jax.ShapeDtypeStruct((piece, local_width), f32),
                jax.ShapeDtypeStruct((3, piece, local_width), f32),
            ],
            mine.size,
            mine,
            swap(theirs),
        )
        return (grad_qkv, grad_attn_out.T, grad_projector.T)

    return local


def solution(mesh):
    placed = (
        P("wide", "narrow"),
        P("narrow"),
        P("narrow", "wide"),
        P("wide", "narrow"),
        P("narrow", "wide"),
        P("wide", None, None),
        P("wide", None),
        P(None, None, "narrow"),
        P("narrow", None),
    )
    return jax.shard_map(
        make_local(mesh.shape["wide"], mesh.shape["narrow"]),
        mesh=mesh,
        in_specs=placed,
        out_specs=(P(None, "wide", "narrow"), P("narrow", "wide"), P("narrow", "wide")),
        check_vma=False,
    )
```

```python
import functools

import jax
import jax.numpy as jnp
import numpy as np
from jax import lax
from jax.experimental import pallas as pl
from jax.experimental.pallas import tpu as pltpu
from jax.sharding import PartitionSpec as P

HEAD_DIM = 64
LANES = 128
EPSILON = 1e-06
CORES = 2

f32 = jnp.float32
bf16 = jnp.bfloat16


def product(left, right, dims=((1,), (0,))):
    return lax.dot_general(left, right, (dims, ((), ())), preferred_element_type=f32)


def chip_groups(wide, cores):
    return [[chip * cores + c for chip in range(wide // cores)] for c in range(cores)]


def exchange(block, axis, groups=None):
    return lax.all_to_all(block, axis, 0, 0, axis_index_groups=groups)


def spread(block, axis, count, groups=None):
    return exchange(jnp.broadcast_to(block[None], (count,) + block.shape), axis, groups)


def by_head(block, heads):
    lane_head = lax.broadcasted_iota(jnp.int32, block.shape, 1) // HEAD_DIM
    return jnp.concatenate([jnp.where(lane_head == h, block, 0.0) for h in range(heads)], axis=0)


def merge_heads(block, heads):
    picks = block.shape[0] // heads
    merged = block[:picks]
    lane_head = lax.broadcasted_iota(jnp.int32, merged.shape, 1) // HEAD_DIM
    for h in range(1, heads):
        merged = jnp.where(lane_head == h, block[h * picks : (h + 1) * picks], merged)
    return merged


def rounded(block):
    return block.astype(bf16).astype(f32)


def forward_kernel(
    patches,
    wanted_ref,
    first_ref,
    student_ref,
    w_qkv_ref,
    w_out_ref,
    norm_ref,
    keys_ref,
    values_ref,
    probs_ref,
    side_ref,
    early_ref,
    picked_norm_ref,
    picked_in_ref,
    mixed_ref,
):
    total, width = student_ref.shape
    heads = keys_ref.shape[1] // HEAD_DIM
    for start in range(0, total, patches):
        at = pl.ds(start, patches)
        source = student_ref[at, :].astype(f32)
        center = jnp.mean(source, axis=1, keepdims=True)
        spread_s = jnp.mean(source * source, axis=1, keepdims=True) - center * center
        norm = ((source - center) * lax.rsqrt(spread_s + EPSILON)).astype(bf16)
        norm_ref[at, :] = norm
        keys_ref[at, :] = product(norm, w_qkv_ref[1]).astype(bf16)
        values_ref[at, :] = product(norm, w_qkv_ref[2]).astype(bf16)
    norm = norm_ref[...]
    picks = wanted_ref.shape[0]
    column = lax.broadcasted_iota(jnp.int32, (picks, total), 1)
    chosen = jnp.where(column == wanted_ref[...], 1.0, 0.0).astype(bf16)
    picked_norm = product(chosen, norm)
    picked_norm_ref[...] = picked_norm
    picked_in_ref[...] = product(chosen, student_ref[...])
    queries = product(picked_norm.astype(bf16), w_qkv_ref[0])
    scores = product(by_head(queries, heads).astype(bf16), keys_ref[...], ((1,), (1,)))
    column = lax.broadcasted_iota(jnp.int32, scores.shape, 1)
    first = first_ref[...]
    inside = (column >= first) & (column < first + patches)
    scores = jnp.where(inside, scores * HEAD_DIM ** (-0.5), -jnp.inf)
    top = jnp.max(scores, axis=1, keepdims=True)
    powers = jnp.where(inside, jnp.exp(scores - top), 0.0)
    probs = powers / jnp.sum(powers, axis=1, keepdims=True)
    probs_ref[...] = probs
    probs_low = probs.astype(bf16)
    context = merge_heads(product(probs_low, values_ref[...]), heads)
    side_ref[...] = product(probs_low, norm)
    early_ref[...] = jnp.concatenate([queries, context], axis=1)
    mixed_ref[...] = product(context.astype(bf16), w_out_ref[...])


def backward_kernel(
    divisor,
    terms_ref,
    picked_in_ref,
    probs_ref,
    keys_ref,
    values_ref,
    norm_ref,
    w_out_ref,
    picked_norm_ref,
    side_ref,
    early_ref,
    teacher_ref,
    move_ref,
    send_ref,
):
    picks, width = picked_in_ref.shape
    local_width = keys_ref.shape[1]
    heads = local_width // HEAD_DIM
    delta = (picked_in_ref[...] + jnp.sum(terms_ref[...].astype(f32), axis=0)) / divisor
    d_context = product(delta.astype(bf16), w_out_ref[...], ((1,), (1,)))
    d_probs = product(by_head(d_context, heads).astype(bf16), values_ref[...], ((1,), (1,)))
    probs = probs_ref[...]
    held = jnp.sum(probs * d_probs, axis=1, keepdims=True)
    d_scores = (probs * (d_probs - held) * HEAD_DIM ** (-0.5)).astype(bf16)
    d_query = merge_heads(product(d_scores, keys_ref[...]), heads)
    key_side = product(d_scores, norm_ref[...])
    shared = jnp.concatenate(
        [teacher_ref[...].astype(f32), early_ref[...], d_query, d_context], axis=1
    )
    shared_width = shared.shape[1]
    twice = jnp.concatenate([shared, shared], axis=0).astype(bf16)
    for start in range(0, send_ref.shape[0], 2 * picks):
        send_ref[pl.ds(start, 2 * picks), pl.ds(0, shared_width)] = twice

    side = side_ref[...]
    factors = [delta, picked_norm_ref[...]]
    factors += [key_side[h * picks : (h + 1) * picks] for h in range(heads)]
    factors += [side[h * picks : (h + 1) * picks] for h in range(heads)]
    lines = [
        jnp.concatenate([factor[:, at : at + LANES] for factor in factors], axis=1)
        for at in range(0, width, LANES)
    ]
    packed = product(jnp.concatenate(lines, axis=0).astype(bf16), move_ref[...])
    per_tile = packed.shape[1] // LANES
    chips_per_tile = per_tile // CORES
    for chip in range(0, send_ref.shape[0] // picks, 2):
        tile, place = chip // chips_per_tile, chip % chips_per_tile
        for core in range(CORES):
            pieces = []
            for spot in (place, place + 1):
                lane = (spot * CORES + core) * LANES
                pieces.append(packed[tile * picks : (tile + 1) * picks, lane : lane + LANES])
            send_ref[
                pl.ds(chip * picks, 2 * picks), pl.ds(shared_width + core * LANES, LANES)
            ] = jnp.concatenate(pieces, axis=0).astype(bf16)


def thirds(block):
    high = rounded(block)
    middle = rounded(block - high)
    return [high, middle, block - high - middle]


def first_kernel(rows_ref, columns_ref, send_ref):
    block = jnp.concatenate([rows_ref[...].astype(f32), columns_ref[...].astype(f32)], axis=0)
    block = block.astype(bf16)
    for n in range(send_ref.shape[0]):
        send_ref[n] = block


def up_kernel(own_ref, other_ref, gain_ref, weight_ref, send_ref):
    parts, _, hidden = send_ref.shape
    size = own_ref.shape[0] // parts
    features = own_ref.shape[1]
    pieces = []
    for n in range(parts):
        pieces += [own_ref[pl.ds(n * size, size), :], other_ref[pl.ds(n * size, size), :]]
    low = jnp.concatenate(pieces, axis=0)
    rows = low.astype(f32)
    gain = gain_ref[...].astype(f32)
    center = jnp.mean(rows, axis=1, keepdims=True)
    pre = product(((rows - center) * gain).astype(bf16), weight_ref[...]).astype(bf16)
    total = jnp.sum(rows * rows, axis=1, keepdims=True)
    lane = lax.broadcasted_iota(jnp.int32, (rows.shape[0], LANES), 1)
    lines = jnp.where(lane == 0, center, jnp.where(lane == 1, total, 0.0)).T
    means, totals = lines[0:1], lines[1:2]
    stats = jnp.concatenate(thirds(means) + thirds(totals), axis=0)
    gains = product(jnp.broadcast_to(gain, (8, features)).astype(bf16), weight_ref[...])[0:1]
    gains = jnp.concatenate(thirds(gains), axis=0)
    span = 2 * size
    for n in range(parts):
        send_ref[n, pl.ds(0, span), :] = pre[n * span : (n + 1) * span]
        tile = n * span // LANES * LANES
        mine = stats[:, tile : tile + LANES]
        if n * span % LANES:
            mine = pltpu.roll(mine, LANES - n * span % LANES, 1)
        lines = [mine] + [jnp.zeros_like(mine)] * (hidden // LANES - 1)
        extra = jnp.concatenate([gains, jnp.concatenate(lines, axis=1)], axis=0)
        extra = jnp.concatenate([extra, jnp.zeros((16 - extra.shape[0], hidden), f32)], axis=0)
        send_ref[n, pl.ds(span, 16), :] = extra.astype(bf16)


def gelu_kernel(d_t, parts_ref, send_ref):
    parts, span, _ = send_ref.shape
    pre = parts_ref[0, pl.ds(0, span), :].astype(f32)
    for n in range(1, parts):
        pre = pre + parts_ref[n, pl.ds(0, span), :].astype(f32)
    extra = [parts_ref[n, pl.ds(span, 16), :].astype(f32) for n in range(parts)]

    def joined(block, at):
        return block[at : at + 1] + block[at + 1 : at + 2] + block[at + 2 : at + 3]

    means = [joined(block, 3)[:, :LANES] for block in extra]
    center = sum(means) / parts
    variance = sum(joined(block, 6)[:, :LANES] for block in extra) / d_t - center * center
    lines = [mean - center for mean in means] + [lax.rsqrt(variance + EPSILON)]
    lines = jnp.concatenate(lines + [jnp.zeros((LANES - parts - 1, LANES), f32)], axis=0)
    lines = lines.T[:span]
    for n in range(parts):
        pre = pre + lines[:, n : n + 1] * joined(extra[n], 0)
    pre = pre * lines[:, parts : parts + 1]
    hidden = (0.5 * pre * (1.0 + lax.erf(pre * 0.5**0.5))).astype(bf16)
    for n in range(parts):
        send_ref[n] = hidden


def hidden_half(hidden_ref, place):
    size = hidden_ref.shape[1] // 2
    parts = [hidden_ref[n, pl.ds(place * size, size), :] for n in range(hidden_ref.shape[0])]
    return jnp.concatenate(parts, axis=0)


def down_other_kernel(hidden_ref, weight_ref, out_ref):
    out_ref[...] = product(hidden_half(hidden_ref, 1), weight_ref[...]).astype(bf16)


def down_own_kernel(hidden_ref, weight_ref, add_ref, out_ref):
    own = product(hidden_half(hidden_ref, 0), weight_ref[...])
    out_ref[...] = (own + add_ref[...].astype(f32)).astype(bf16)


def target_kernel(branch_ref, teacher_ref, columns_ref, mixed_ref, local_ref, terms_ref):
    teacher = teacher_ref[...].astype(f32) + jnp.sum(branch_ref[...].astype(f32), axis=0)
    teacher = teacher.astype(bf16)
    local_ref[...] = teacher
    term = mixed_ref[...] - product(teacher, columns_ref[...], ((1,), (1,)))
    term = term.astype(bf16)
    for n in range(terms_ref.shape[0]):
        terms_ref[n] = term


def partial_kernel(piece, features, local_width, core_ref, got_ref, mine_ref, theirs_ref):
    heads = local_width // HEAD_DIM
    shared_width = got_ref.shape[1] - CORES * LANES
    shared = got_ref[:, :shared_width]
    starts = [features + n * local_width for n in range(4)]
    both = []
    for core in range(CORES):
        factors = got_ref[:, shared_width + core * LANES : shared_width + (core + 1) * LANES]
        full = product(factors, shared, ((0,), (0,)))

        def part(kind, start, size):
            return full[kind * piece : (kind + 1) * piece, start : start + size]

        def per_head(kind, start):
            block = part(kind, start, local_width)
            head = lax.broadcasted_iota(jnp.int32, block.shape, 1) // HEAD_DIM
            for h in range(1, heads):
                block = jnp.where(head == h, part(kind + h, start, local_width), block)
            return block

        both.append(
            jnp.concatenate(
                [
                    -part(0, 0, features),
                    part(0, starts[1], local_width),
                    part(1, starts[2], local_width),
                    per_head(2, starts[0]),
                    per_head(2 + heads, starts[3]),
                ],
                axis=1,
            )
        )
    first = core_ref[...] == 0
    mine_ref[...] = jnp.where(first, both[0], both[1])
    theirs_ref[...] = jnp.where(first, both[1], both[0])


def total_kernel(mine_ref, other_ref, projector_ref, attn_ref, qkv_ref):
    total = mine_ref[...] + other_ref[...]
    features, local_width = projector_ref.shape[1], attn_ref.shape[1]
    projector_ref[...] = total[:, :features]
    attn_ref[...] = total[:, features : features + local_width]
    for n in range(3):
        start = features + (n + 1) * local_width
        qkv_ref[n] = total[:, start : start + local_width]


def call_kernel(kernel, out_shape, flops, *operands):
    whole = pl.BlockSpec(memory_space=pltpu.VMEM)
    moved = sum(x.size * x.dtype.itemsize for x in operands)
    return pl.pallas_call(
        kernel,
        out_shape=out_shape,
        in_specs=[whole] * len(operands),
        out_specs=jax.tree.map(lambda _: whole, out_shape),
        compiler_params=pltpu.CompilerParams(vmem_limit_bytes=40 * 2**20),
        cost_estimate=pl.CostEstimate(flops=flops, bytes_accessed=moved, transcendentals=0),
    )(*operands)


def lane_moves(kinds, piece):
    per_tile = LANES // piece
    move = np.zeros((kinds, LANES, per_tile, LANES), np.float32)
    for kind in range(kinds):
        for tile in range(per_tile):
            for lane in range(piece):
                move[kind, tile * piece + lane, tile, kind * piece + lane] = 1.0
    return move.reshape(kinds * LANES, per_tile * LANES)


def make_local(wide, narrow):
    chips = wide // CORES
    groups = chip_groups(wide, CORES)
    pairs = [(i, i ^ 1) for i in range(wide)]

    def swap(block):
        return lax.ppermute(block, "wide", pairs)

    def doubled(blocks, bit):
        other = lax.ppermute(blocks, "wide", [(i, i ^ bit) for i in range(wide)])
        mine = (lax.axis_index("wide") & bit != 0).astype(jnp.int32)
        place = lax.broadcasted_iota(jnp.int32, (1, 2) + blocks.shape[1:], 1)
        both = jnp.where(place == mine, blocks[:, None], other[:, None])
        return both.reshape((-1,) + blocks.shape[1:])

    def local(
        teacher_in,
        teacher_gain,
        mlp_in,
        mlp_out,
        projector,
        student_in,
        sample_pos,
        w_qkv,
        w_attn_out,
    ):
        rows, features = teacher_in.shape
        d_t = features * narrow
        images, patches, width = student_in.shape
        select = sample_pos.shape[1]
        local_width = w_qkv.shape[2]
        half = rows * chips
        heads_here = local_width // HEAD_DIM
        picks = images * select

        image_first = np.repeat(np.arange(images, dtype=np.int32) * patches, select)[:, None]
        flat_in = student_in.reshape(images * patches, width)
        norm_shape = jax.ShapeDtypeStruct(flat_in.shape, bf16)
        head_shape = jax.ShapeDtypeStruct((flat_in.shape[0], local_width), bf16)
        score_shape = jax.ShapeDtypeStruct((heads_here * picks, flat_in.shape[0]), f32)
        side_shape = jax.ShapeDtypeStruct((heads_here * picks, width), f32)
        early_shape = jax.ShapeDtypeStruct((picks, 2 * local_width), f32)
        row_shape = jax.ShapeDtypeStruct((picks, width), f32)
        student = call_kernel(
            functools.partial(forward_kernel, patches),
            [norm_shape, head_shape, head_shape, score_shape, side_shape, early_shape]
            + [row_shape] * 3,
            2 * flat_in.size * (2 * local_width + 4 * picks),
            sample_pos.reshape(picks, 1) + image_first,
            jnp.asarray(np.tile(image_first, (heads_here, 1))),
            flat_in,
            w_qkv,
            w_attn_out,
        )

        piece = width // wide
        first = call_kernel(
            first_kernel,
            jax.ShapeDtypeStruct((chips, rows + piece, features), bf16),
            chips * (rows + piece) * features,
            teacher_in,
            projector.T,
        )
        first = exchange(first, "wide", groups)
        core = (lax.axis_index("wide") % CORES).reshape(1, 1)
        first, student, core = lax.optimization_barrier((first, student, core))
        norm, keys, values, probs, side, early, picked_norm, picked_in, mixed = student
        raw = first[:, :rows].reshape(half, features)
        raw_other = swap(raw)

        hidden_shape = jax.ShapeDtypeStruct((narrow, 2 * half // narrow, mlp_in.shape[1]), bf16)
        rows_shape = jax.ShapeDtypeStruct((half, features), bf16)
        up_flops = 4 * half * mlp_in.size
        pre = call_kernel(
            up_kernel,
            jax.ShapeDtypeStruct((narrow, 2 * half // narrow + 16, mlp_in.shape[1]), bf16),
            up_flops,
            raw,
            raw_other,
            teacher_gain.reshape(1, features),
            mlp_in,
        )
        columns = doubled(first[:, rows:], 1).reshape(-1, features)
        pre = exchange(pre, "narrow")
        hidden = call_kernel(functools.partial(gelu_kernel, d_t), hidden_shape, 8 * pre.size, pre)
        hidden = exchange(hidden, "narrow")
        hidden, columns = lax.optimization_barrier((hidden, columns))
        branch = swap(call_kernel(down_other_kernel, rows_shape, up_flops // 2, hidden, mlp_out))
        branch = call_kernel(
            down_own_kernel, rows_shape, up_flops // 2, hidden, mlp_out, branch
        )
        branch = exchange(branch.reshape(chips, rows, features), "wide", groups)
        teacher_local, terms = call_kernel(
            target_kernel,
            [
                jax.ShapeDtypeStruct((rows, features), bf16),
                jax.ShapeDtypeStruct((narrow, picks, width), bf16),
            ],
            2 * rows * columns.size,
            branch,
            teacher_in,
            columns,
            mixed,
        )
        terms = exchange(terms, "narrow")

        kinds = 2 + 2 * heads_here
        shared_width = features + 4 * local_width
        got = call_kernel(
            functools.partial(backward_kernel, float(select * images)),
            jax.ShapeDtypeStruct((half, shared_width + CORES * LANES), bf16),
            2 * norm.size * heads_here * picks,
            terms,
            picked_in,
            probs,
            keys,
            values,
            norm,
            w_attn_out,
            picked_norm,
            side,
            early,
            teacher_local,
            jnp.asarray(lane_moves(kinds, piece), bf16),
        )
        got = exchange(got.reshape(chips, rows, -1), "wide", groups).reshape(half, -1)
        totals_shape = jax.ShapeDtypeStruct((piece, shared_width), f32)
        mine, theirs = call_kernel(
            functools.partial(partial_kernel, piece, features, local_width),
            [totals_shape, totals_shape],
            4 * LANES * half * shared_width,
            core,
            got,
        )
        grad_projector, grad_attn_out, grad_qkv = call_kernel(
            total_kernel,
            [
                jax.ShapeDtypeStruct((piece, features), f32),
                jax.ShapeDtypeStruct((piece, local_width), f32),
                jax.ShapeDtypeStruct((3, piece, local_width), f32),
            ],
            mine.size,
            mine,
            swap(theirs),
        )
        return (grad_qkv, grad_attn_out.T, grad_projector.T)

    return local


def solution(mesh):
    placed = (
        P("wide", "narrow"),
        P("narrow"),
        P("narrow", "wide"),
        P("wide", "narrow"),
        P("narrow", "wide"),
        P("wide", None, None),
        P("wide", None),
        P(None, None, "narrow"),
        P("narrow", None),
    )
    return jax.shard_map(
        make_local(mesh.shape["wide"], mesh.shape["narrow"]),
        mesh=mesh,
        in_specs=placed,
        out_specs=(P(None, "wide", "narrow"), P("narrow", "wide"), P("narrow", "wide")),
        check_vma=False,
    )
```

```python
import functools

import jax
import jax.numpy as jnp
import numpy as np
from jax import lax
from jax.experimental import pallas as pl
from jax.experimental.pallas import tpu as pltpu
from jax.sharding import PartitionSpec as P

HEAD_DIM = 64
LANES = 128
EPSILON = 1e-06
CORES = 2

f32 = jnp.float32
bf16 = jnp.bfloat16


def product(left, right, dims=((1,), (0,))):
    return lax.dot_general(left, right, (dims, ((), ())), preferred_element_type=f32)


def chip_groups(wide, cores):
    return [[chip * cores + c for chip in range(wide // cores)] for c in range(cores)]


def exchange(block, axis, groups=None):
    return lax.all_to_all(block, axis, 0, 0, axis_index_groups=groups)


def spread(block, axis, count, groups=None):
    return exchange(jnp.broadcast_to(block[None], (count,) + block.shape), axis, groups)


def by_head(block, heads):
    lane_head = lax.broadcasted_iota(jnp.int32, block.shape, 1) // HEAD_DIM
    return jnp.concatenate([jnp.where(lane_head == h, block, 0.0) for h in range(heads)], axis=0)


def merge_heads(block, heads):
    picks = block.shape[0] // heads
    merged = block[:picks]
    lane_head = lax.broadcasted_iota(jnp.int32, merged.shape, 1) // HEAD_DIM
    for h in range(1, heads):
        merged = jnp.where(lane_head == h, block[h * picks : (h + 1) * picks], merged)
    return merged


def rounded(block):
    return block.astype(bf16).astype(f32)


def forward_kernel(
    patches,
    wanted_ref,
    first_ref,
    student_ref,
    w_qkv_ref,
    w_out_ref,
    norm_ref,
    keys_ref,
    values_ref,
    probs_ref,
    side_ref,
    early_ref,
    picked_norm_ref,
    picked_in_ref,
    mixed_ref,
):
    total, width = student_ref.shape
    heads = keys_ref.shape[1] // HEAD_DIM
    for start in range(0, total, patches):
        at = pl.ds(start, patches)
        source = student_ref[at, :].astype(f32)
        center = jnp.mean(source, axis=1, keepdims=True)
        spread_s = jnp.mean(source * source, axis=1, keepdims=True) - center * center
        norm = ((source - center) * lax.rsqrt(spread_s + EPSILON)).astype(bf16)
        norm_ref[at, :] = norm
        keys_ref[at, :] = product(norm, w_qkv_ref[1]).astype(bf16)
        values_ref[at, :] = product(norm, w_qkv_ref[2]).astype(bf16)
    norm = norm_ref[...]
    picks = wanted_ref.shape[0]
    column = lax.broadcasted_iota(jnp.int32, (picks, total), 1)
    chosen = jnp.where(column == wanted_ref[...], 1.0, 0.0).astype(bf16)
    picked_norm = product(chosen, norm)
    picked_norm_ref[...] = picked_norm
    picked_in_ref[...] = product(chosen, student_ref[...])
    queries = product(picked_norm.astype(bf16), w_qkv_ref[0])
    scores = product(by_head(queries, heads).astype(bf16), keys_ref[...], ((1,), (1,)))
    column = lax.broadcasted_iota(jnp.int32, scores.shape, 1)
    first = first_ref[...]
    inside = (column >= first) & (column < first + patches)
    scores = jnp.where(inside, scores * HEAD_DIM ** (-0.5), -jnp.inf)
    top = jnp.max(scores, axis=1, keepdims=True)
    powers = jnp.where(inside, jnp.exp(scores - top), 0.0)
    probs = powers / jnp.sum(powers, axis=1, keepdims=True)
    probs_ref[...] = probs
    probs_low = probs.astype(bf16)
    context = merge_heads(product(probs_low, values_ref[...]), heads)
    side_ref[...] = product(probs_low, norm)
    early_ref[...] = jnp.concatenate([queries, context], axis=1)
    mixed_ref[...] = product(context.astype(bf16), w_out_ref[...])


def backward_kernel(
    divisor,
    terms_ref,
    picked_in_ref,
    probs_ref,
    keys_ref,
    values_ref,
    norm_ref,
    w_out_ref,
    picked_norm_ref,
    side_ref,
    early_ref,
    teacher_ref,
    move_ref,
    send_ref,
):
    picks, width = picked_in_ref.shape
    local_width = keys_ref.shape[1]
    heads = local_width // HEAD_DIM
    delta = (picked_in_ref[...] + jnp.sum(terms_ref[...].astype(f32), axis=0)) / divisor
    d_context = product(delta.astype(bf16), w_out_ref[...], ((1,), (1,)))
    d_probs = product(by_head(d_context, heads).astype(bf16), values_ref[...], ((1,), (1,)))
    probs = probs_ref[...]
    held = jnp.sum(probs * d_probs, axis=1, keepdims=True)
    d_scores = (probs * (d_probs - held) * HEAD_DIM ** (-0.5)).astype(bf16)
    d_query = merge_heads(product(d_scores, keys_ref[...]), heads)
    key_side = product(d_scores, norm_ref[...])
    shared = jnp.concatenate(
        [teacher_ref[...].astype(f32), early_ref[...], d_query, d_context], axis=1
    )
    shared_width = shared.shape[1]
    twice = jnp.concatenate([shared, shared], axis=0).astype(bf16)
    for start in range(0, send_ref.shape[0], 2 * picks):
        send_ref[pl.ds(start, 2 * picks), pl.ds(0, shared_width)] = twice

    side = side_ref[...]
    factors = [delta, picked_norm_ref[...]]
    factors += [key_side[h * picks : (h + 1) * picks] for h in range(heads)]
    factors += [side[h * picks : (h + 1) * picks] for h in range(heads)]
    lines = [
        jnp.concatenate([factor[:, at : at + LANES] for factor in factors], axis=1)
        for at in range(0, width, LANES)
    ]
    packed = product(jnp.concatenate(lines, axis=0).astype(bf16), move_ref[...])
    per_tile = packed.shape[1] // LANES
    chips_per_tile = per_tile // CORES
    for chip in range(0, send_ref.shape[0] // picks, 2):
        tile, place = chip // chips_per_tile, chip % chips_per_tile
        for core in range(CORES):
            pieces = []
            for spot in (place, place + 1):
                lane = (spot * CORES + core) * LANES
                pieces.append(packed[tile * picks : (tile + 1) * picks, lane : lane + LANES])
            send_ref[
                pl.ds(chip * picks, 2 * picks), pl.ds(shared_width + core * LANES, LANES)
            ] = jnp.concatenate(pieces, axis=0).astype(bf16)


def thirds(block):
    high = rounded(block)
    middle = rounded(block - high)
    return [high, middle, block - high - middle]


def first_kernel(rows_ref, columns_ref, send_ref):
    block = jnp.concatenate([rows_ref[...].astype(f32), columns_ref[...].astype(f32)], axis=0)
    block = block.astype(bf16)
    for n in range(send_ref.shape[0]):
        send_ref[n] = block


def up_half(rows_ref, gain, weight_ref):
    rows = rows_ref[...].astype(f32)
    center = jnp.mean(rows, axis=1, keepdims=True)
    pre = product(((rows - center) * gain).astype(bf16), weight_ref[...]).astype(bf16)
    total = jnp.sum(rows * rows, axis=1, keepdims=True)
    lane = lax.broadcasted_iota(jnp.int32, (rows.shape[0], LANES), 1)
    lines = jnp.where(lane == 0, center, jnp.where(lane == 1, total, 0.0)).T
    return pre, lines[:8]


def up_own_kernel(rows_ref, gain_ref, weight_ref, pre_ref, lines_ref, gains_ref):
    gain = gain_ref[...].astype(f32)
    pre, lines = up_half(rows_ref, gain, weight_ref)
    pre_ref[...] = pre
    lines_ref[...] = lines
    gain = jnp.broadcast_to(gain, (8, gain.shape[1])).astype(bf16)
    gains_ref[...] = product(gain, weight_ref[...])


def up_kernel(rows_ref, gain_ref, weight_ref, own_ref, own_lines_ref, gains_ref, send_ref):
    parts, _, hidden = send_ref.shape
    size = own_ref.shape[0] // parts
    pre, lines = up_half(rows_ref, gain_ref[...].astype(f32), weight_ref)
    gains = jnp.concatenate(thirds(gains_ref[0:1, :]), axis=0)
    stats = []
    for held in (own_lines_ref[...], lines):
        stats.append(jnp.concatenate(thirds(held[0:1]) + thirds(held[1:2]), axis=0))
    for n in range(parts):
        send_ref[n, pl.ds(0, size), :] = own_ref[pl.ds(n * size, size), :]
        send_ref[n, pl.ds(size, size), :] = pre[n * size : (n + 1) * size]
        tile, shift = n * size // LANES * LANES, n * size % LANES
        own, other = [block[:, tile : tile + LANES] for block in stats]
        if shift:
            own = pltpu.roll(own, LANES - shift, 1)
        if shift != size:
            other = pltpu.roll(other, (LANES + size - shift) % LANES, 1)
        lane = lax.broadcasted_iota(jnp.int32, own.shape, 1)
        mine = jnp.where(lane < size, own, other)
        line = [mine] + [jnp.zeros_like(mine)] * (hidden // LANES - 1)
        extra = jnp.concatenate([gains, jnp.concatenate(line, axis=1)], axis=0)
        extra = jnp.concatenate([extra, jnp.zeros((16 - extra.shape[0], hidden), f32)], axis=0)
        send_ref[n, pl.ds(2 * size, 16), :] = extra.astype(bf16)


def gelu_kernel(d_t, parts_ref, send_ref):
    parts, span, _ = send_ref.shape
    pre = parts_ref[0, pl.ds(0, span), :].astype(f32)
    for n in range(1, parts):
        pre = pre + parts_ref[n, pl.ds(0, span), :].astype(f32)
    extra = [parts_ref[n, pl.ds(span, 16), :].astype(f32) for n in range(parts)]

    def joined(block, at):
        return block[at : at + 1] + block[at + 1 : at + 2] + block[at + 2 : at + 3]

    means = [joined(block, 3)[:, :LANES] for block in extra]
    center = sum(means) / parts
    variance = sum(joined(block, 6)[:, :LANES] for block in extra) / d_t - center * center
    lines = [mean - center for mean in means] + [lax.rsqrt(variance + EPSILON)]
    lines = jnp.concatenate(lines + [jnp.zeros((LANES - parts - 1, LANES), f32)], axis=0)
    lines = lines.T[:span]
    for n in range(parts):
        pre = pre + lines[:, n : n + 1] * joined(extra[n], 0)
    pre = pre * lines[:, parts : parts + 1]
    hidden = (0.5 * pre * (1.0 + lax.erf(pre * 0.5**0.5))).astype(bf16)
    for n in range(parts):
        send_ref[n] = hidden


def hidden_half(hidden_ref, place):
    size = hidden_ref.shape[1] // 2
    parts = [hidden_ref[n, pl.ds(place * size, size), :] for n in range(hidden_ref.shape[0])]
    return jnp.concatenate(parts, axis=0)


def down_other_kernel(hidden_ref, weight_ref, out_ref):
    out_ref[...] = product(hidden_half(hidden_ref, 1), weight_ref[...]).astype(bf16)


def down_own_kernel(hidden_ref, weight_ref, add_ref, out_ref):
    own = product(hidden_half(hidden_ref, 0), weight_ref[...])
    out_ref[...] = (own + add_ref[...].astype(f32)).astype(bf16)


def target_kernel(branch_ref, teacher_ref, columns_ref, mixed_ref, local_ref, terms_ref):
    teacher = teacher_ref[...].astype(f32) + jnp.sum(branch_ref[...].astype(f32), axis=0)
    teacher = teacher.astype(bf16)
    local_ref[...] = teacher
    term = mixed_ref[...] - product(teacher, columns_ref[...], ((1,), (1,)))
    term = term.astype(bf16)
    for n in range(terms_ref.shape[0]):
        terms_ref[n] = term


def partial_kernel(piece, features, local_width, core_ref, got_ref, mine_ref, theirs_ref):
    heads = local_width // HEAD_DIM
    shared_width = got_ref.shape[1] - CORES * LANES
    shared = got_ref[:, :shared_width]
    starts = [features + n * local_width for n in range(4)]
    both = []
    for core in range(CORES):
        factors = got_ref[:, shared_width + core * LANES : shared_width + (core + 1) * LANES]
        full = product(factors, shared, ((0,), (0,)))

        def part(kind, start, size):
            return full[kind * piece : (kind + 1) * piece, start : start + size]

        def per_head(kind, start):
            block = part(kind, start, local_width)
            head = lax.broadcasted_iota(jnp.int32, block.shape, 1) // HEAD_DIM
            for h in range(1, heads):
                block = jnp.where(head == h, part(kind + h, start, local_width), block)
            return block

        both.append(
            jnp.concatenate(
                [
                    -part(0, 0, features),
                    part(0, starts[1], local_width),
                    part(1, starts[2], local_width),
                    per_head(2, starts[0]),
                    per_head(2 + heads, starts[3]),
                ],
                axis=1,
            )
        )
    first = core_ref[...] == 0
    mine_ref[...] = jnp.where(first, both[0], both[1])
    theirs_ref[...] = jnp.where(first, both[1], both[0])


def total_kernel(mine_ref, other_ref, projector_ref, attn_ref, qkv_ref):
    total = mine_ref[...] + other_ref[...]
    features, local_width = projector_ref.shape[1], attn_ref.shape[1]
    projector_ref[...] = total[:, :features]
    attn_ref[...] = total[:, features : features + local_width]
    for n in range(3):
        start = features + (n + 1) * local_width
        qkv_ref[n] = total[:, start : start + local_width]


def call_kernel(kernel, out_shape, flops, *operands):
    whole = pl.BlockSpec(memory_space=pltpu.VMEM)
    moved = sum(x.size * x.dtype.itemsize for x in operands)
    return pl.pallas_call(
        kernel,
        out_shape=out_shape,
        in_specs=[whole] * len(operands),
        out_specs=jax.tree.map(lambda _: whole, out_shape),
        compiler_params=pltpu.CompilerParams(vmem_limit_bytes=40 * 2**20),
        cost_estimate=pl.CostEstimate(flops=flops, bytes_accessed=moved, transcendentals=0),
    )(*operands)


def lane_moves(kinds, piece):
    per_tile = LANES // piece
    move = np.zeros((kinds, LANES, per_tile, LANES), np.float32)
    for kind in range(kinds):
        for tile in range(per_tile):
            for lane in range(piece):
                move[kind, tile * piece + lane, tile, kind * piece + lane] = 1.0
    return move.reshape(kinds * LANES, per_tile * LANES)


def make_local(wide, narrow):
    chips = wide // CORES
    groups = chip_groups(wide, CORES)
    pairs = [(i, i ^ 1) for i in range(wide)]

    def swap(block):
        return lax.ppermute(block, "wide", pairs)

    def doubled(blocks, bit):
        other = lax.ppermute(blocks, "wide", [(i, i ^ bit) for i in range(wide)])
        mine = (lax.axis_index("wide") & bit != 0).astype(jnp.int32)
        place = lax.broadcasted_iota(jnp.int32, (1, 2) + blocks.shape[1:], 1)
        both = jnp.where(place == mine, blocks[:, None], other[:, None])
        return both.reshape((-1,) + blocks.shape[1:])

    def local(
        teacher_in,
        teacher_gain,
        mlp_in,
        mlp_out,
        projector,
        student_in,
        sample_pos,
        w_qkv,
        w_attn_out,
    ):
        rows, features = teacher_in.shape
        d_t = features * narrow
        images, patches, width = student_in.shape
        select = sample_pos.shape[1]
        local_width = w_qkv.shape[2]
        half = rows * chips
        heads_here = local_width // HEAD_DIM
        picks = images * select

        image_first = np.repeat(np.arange(images, dtype=np.int32) * patches, select)[:, None]
        flat_in = student_in.reshape(images * patches, width)
        norm_shape = jax.ShapeDtypeStruct(flat_in.shape, bf16)
        head_shape = jax.ShapeDtypeStruct((flat_in.shape[0], local_width), bf16)
        score_shape = jax.ShapeDtypeStruct((heads_here * picks, flat_in.shape[0]), f32)
        side_shape = jax.ShapeDtypeStruct((heads_here * picks, width), f32)
        early_shape = jax.ShapeDtypeStruct((picks, 2 * local_width), f32)
        row_shape = jax.ShapeDtypeStruct((picks, width), f32)
        student = call_kernel(
            functools.partial(forward_kernel, patches),
            [norm_shape, head_shape, head_shape, score_shape, side_shape, early_shape]
            + [row_shape] * 3,
            2 * flat_in.size * (2 * local_width + 4 * picks),
            sample_pos.reshape(picks, 1) + image_first,
            jnp.asarray(np.tile(image_first, (heads_here, 1))),
            flat_in,
            w_qkv,
            w_attn_out,
        )

        piece = width // wide
        first = call_kernel(
            first_kernel,
            jax.ShapeDtypeStruct((chips, rows + piece, features), bf16),
            chips * (rows + piece) * features,
            teacher_in,
            projector.T,
        )
        first = exchange(first, "wide", groups)
        core = (lax.axis_index("wide") % CORES).reshape(1, 1)
        first, student, core = lax.optimization_barrier((first, student, core))
        norm, keys, values, probs, side, early, picked_norm, picked_in, mixed = student
        raw = first[:, :rows].reshape(half, features)
        raw_other = swap(raw)

        hidden_shape = jax.ShapeDtypeStruct((narrow, 2 * half // narrow, mlp_in.shape[1]), bf16)
        rows_shape = jax.ShapeDtypeStruct((half, features), bf16)
        up_flops = 4 * half * mlp_in.size
        gain = teacher_gain.reshape(1, features)
        up_own = call_kernel(
            up_own_kernel,
            [
                jax.ShapeDtypeStruct((half, mlp_in.shape[1]), bf16),
                jax.ShapeDtypeStruct((8, half), f32),
                jax.ShapeDtypeStruct((8, mlp_in.shape[1]), f32),
            ],
            up_flops // 2,
            raw,
            gain,
            mlp_in,
        )
        pre = call_kernel(
            up_kernel,
            jax.ShapeDtypeStruct((narrow, 2 * half // narrow + 16, mlp_in.shape[1]), bf16),
            up_flops // 2,
            raw_other,
            gain,
            mlp_in,
            *up_own,
        )
        columns = doubled(first[:, rows:], 1).reshape(-1, features)
        pre = exchange(pre, "narrow")
        hidden = call_kernel(functools.partial(gelu_kernel, d_t), hidden_shape, 8 * pre.size, pre)
        hidden = exchange(hidden, "narrow")
        hidden, columns = lax.optimization_barrier((hidden, columns))
        branch = swap(call_kernel(down_other_kernel, rows_shape, up_flops // 2, hidden, mlp_out))
        branch = call_kernel(
            down_own_kernel, rows_shape, up_flops // 2, hidden, mlp_out, branch
        )
        branch = exchange(branch.reshape(chips, rows, features), "wide", groups)
        teacher_local, terms = call_kernel(
            target_kernel,
            [
                jax.ShapeDtypeStruct((rows, features), bf16),
                jax.ShapeDtypeStruct((narrow, picks, width), bf16),
            ],
            2 * rows * columns.size,
            branch,
            teacher_in,
            columns,
            mixed,
        )
        terms = exchange(terms, "narrow")

        kinds = 2 + 2 * heads_here
        shared_width = features + 4 * local_width
        got = call_kernel(
            functools.partial(backward_kernel, float(select * images)),
            jax.ShapeDtypeStruct((half, shared_width + CORES * LANES), bf16),
            2 * norm.size * heads_here * picks,
            terms,
            picked_in,
            probs,
            keys,
            values,
            norm,
            w_attn_out,
            picked_norm,
            side,
            early,
            teacher_local,
            jnp.asarray(lane_moves(kinds, piece), bf16),
        )
        got = exchange(got.reshape(chips, rows, -1), "wide", groups).reshape(half, -1)
        totals_shape = jax.ShapeDtypeStruct((piece, shared_width), f32)
        mine, theirs = call_kernel(
            functools.partial(partial_kernel, piece, features, local_width),
            [totals_shape, totals_shape],
            4 * LANES * half * shared_width,
            core,
            got,
        )
        grad_projector, grad_attn_out, grad_qkv = call_kernel(
            total_kernel,
            [
                jax.ShapeDtypeStruct((piece, features), f32),
                jax.ShapeDtypeStruct((piece, local_width), f32),
                jax.ShapeDtypeStruct((3, piece, local_width), f32),
            ],
            mine.size,
            mine,
            swap(theirs),
        )
        return (grad_qkv, grad_attn_out.T, grad_projector.T)

    return local


def solution(mesh):
    placed = (
        P("wide", "narrow"),
        P("narrow"),
        P("narrow", "wide"),
        P("wide", "narrow"),
        P("narrow", "wide"),
        P("wide", None, None),
        P("wide", None),
        P(None, None, "narrow"),
        P("narrow", None),
    )
    return jax.shard_map(
        make_local(mesh.shape["wide"], mesh.shape["narrow"]),
        mesh=mesh,
        in_specs=placed,
        out_specs=(P(None, "wide", "narrow"), P("narrow", "wide"), P("narrow", "wide")),
        check_vma=False,
    )
```
